512 devices in a mesh: pop: 16 (over z, y_hi), row: 4 (over y_lo), col: 8 (over x, core).
Axes of the slice: x: 4, y: 8 (y_hi: 2, y_lo: 4; y = y_hi * 4 + y_lo), z: 8, core: 2. Of those that a mesh axis runs over, the one named last changes fastest.
Arguments:
- inputs: bfloat16 [8192, 4096], P(('pop', 'row'), 'col'), may hold values from -6 to 6
- mix: float32 [4096], P('col'), may hold values from 0.05 to 0.95
- key_weight: bfloat16 [4096, 16384], P('col', ('row', 'pop')), may hold values from -0.09375 to 0.09375
- value_weight: bfloat16 [16384, 4096], P(('row', 'pop'), 'col'), may hold values from -0.046875 to 0.046875
- dim_bank: float32 [64, 4096], P(None, 'col'), may hold values from -6 to 6
- hidden_bank: float32 [64, 16384], P(None, 'row'), may hold values from -6 to 6
- member_picks: int32 [128, 4], P(('pop', 'row')), may hold values from 0 to 63
- ranks: int32 [128], P(('pop', 'row')), may hold values from 0 to 127, each once
Outputs:
- outputs: bfloat16 [8192, 4096], P(('pop', 'row'), 'col')
- key_step: float32 [4096, 16384], P('col', ('row', 'pop'))
- value_step: float32 [16384, 4096], P(('row', 'pop'), 'col')
The draws below stay inside these ranges and needn't reach their ends.
Inputs may be any that keep to these rules, and one draw needn't show every extreme that they name: `member_picks`: factor indices into the banks. `ranks`: each rank appears once.
All inputs are finite; a program needn't handle non-finite values.
Results may differ from the reference program's by a relative error of at most 0.022.
Values may be sent and summed in bfloat16 or wider, within the bound.
No kernel may reach another device: no remote copies, remote signals or barrier semaphores. Data moves between devices by JAX's collectives and lax.ppermute only.
A program may use at most 64 MiB of HBM per device.

```python
import jax
import jax.numpy as jnp
from jax import lax

D = 4096
FF = 16384
BATCH = 64
BANK = 64
MEMBERS = 128
TOKENS = 8192
N_COL = 8


def plant(values, stream_key, low, largest):
    longest = values.shape.index(max(values.shape))
    spots = []
    for shift in (0, 1):
        where = [jax.random.randint(jax.random.fold_in(stream_key, axis), (), 0, length) for axis, length in enumerate(values.shape)]
        where[longest] = (where[longest] + shift) % values.shape[longest]
        spots.append(tuple(where))
    return values.at[spots[0]].set(low).at[spots[1]].set(largest)


def block_scale(rng, shape, split, least, largest):
    loudness = 1.0
    for axis_at, shards_of in split:
        draws = jax.random.uniform(jax.random.fold_in(jax.random.fold_in(rng, 6), axis_at), (shards_of,), jnp.float32, least / len(split), largest / len(split))
        loudness = loudness * jnp.repeat(jnp.exp(draws), shape[axis_at] // shards_of).reshape((-1,) + (1,) * (len(shape) - 1 - axis_at))
    return loudness


def scatter_about(key, extent, deviation, bound, split=(), held_as=jnp.bfloat16):
    entries = deviation * jax.random.normal(key, extent, jnp.float32)
    if split:
        entries = entries * block_scale(key, extent, split, -0.22, 0.18)
    return jnp.clip(entries, -bound, bound).astype(held_as)


def setup_inputs(seed: int = 0) -> dict:
    streams_of = jax.random.split(jax.random.key(seed), 9)
    return {
        "inputs": scatter_about(streams_of[0], (TOKENS, D), 1.0, 6.0, ((0, 64), (1, 8))),
        "mix": jnp.clip(0.05 + 0.9 * jax.random.uniform(streams_of[1], (D,), jnp.float32) ** block_scale(streams_of[1], (D,), ((0, 8),), -0.2, 0.2), 0.05, 0.95),
        "key_weight": scatter_about(streams_of[2], (D, FF), D ** -0.5, 0.09375, ((0, 8), (1, 64))),
        "value_weight": scatter_about(streams_of[3], (FF, D), FF ** -0.5, 0.046875, ((0, 64), (1, 8))),
        "dim_bank": scatter_about(streams_of[4], (BANK, D), 1.0, 6.0, ((1, 8),), jnp.float32),
        "hidden_bank": scatter_about(streams_of[5], (BANK, FF), 1.0, 6.0, ((1, 4),), jnp.float32),
        "member_picks": plant(jax.random.randint(streams_of[6], (MEMBERS, 4), 0, BANK), jax.random.fold_in(streams_of[6], 1), 0, BANK - 1).astype(jnp.int32),
        "ranks": jax.random.permutation(streams_of[7], MEMBERS).astype(jnp.int32),
    }


def reference(inputs, mix, key_weight, value_weight, dim_bank, hidden_bank, member_picks, ranks):
    sigma_k = 0.5 / (D ** 0.5)
    sigma_v = 0.5 / (FF ** 0.5)
    block = D // N_COL
    values = inputs.astype(jnp.float32).reshape(MEMBERS, BATCH, D)
    previous = jnp.concatenate([jnp.zeros((MEMBERS, 1, D), jnp.float32), values[:, :-1, :]], axis=1)
    shifted = (values + (previous - values) * mix).astype(jnp.bfloat16)
    fac_a = jnp.take(dim_bank, member_picks[:, 0], axis=0)
    fac_b = jnp.take(hidden_bank, member_picks[:, 1], axis=0)
    fac_c = jnp.take(hidden_bank, member_picks[:, 2], axis=0)
    fac_d = jnp.take(dim_bank, member_picks[:, 3], axis=0)
    key_full = key_weight.astype(jnp.float32).reshape(N_COL, block, FF)
    value_full = value_weight.astype(jnp.float32)

    def member(items):
        tokens, vec_a, vec_b, vec_c, vec_d = items
        pieces = tokens.astype(jnp.float32).reshape(BATCH, N_COL, block)
        parts = jnp.einsum("tcj,cjf->ctf", pieces, key_full, precision=lax.Precision.HIGHEST)
        inner = jnp.sum(pieces * vec_a.reshape(N_COL, block), axis=-1)
        parts = parts + sigma_k * jnp.transpose(inner)[:, :, None] * vec_b
        parts = lax.optimization_barrier(parts.astype(jnp.bfloat16))
        key_pre = jnp.sum(parts.astype(jnp.float32), axis=0)
        keys = (jnp.maximum(key_pre, 0.0) ** 2).astype(jnp.bfloat16)
        keys_wide = keys.astype(jnp.float32)
        base = jnp.dot(keys_wide, value_full, precision=lax.Precision.HIGHEST)
        inner_c = jnp.sum(keys_wide * vec_c, axis=-1)
        return (base + sigma_v * inner_c[:, None] * vec_d).astype(jnp.bfloat16)

    outputs = lax.map(member, (shifted, fac_a, fac_b, fac_c, fac_d)).reshape(TOKENS, D)
    fitness = 2.0 * ranks.astype(jnp.float32) / (MEMBERS - 1) - 1.0
    scale = 1.0 / (MEMBERS ** 0.5)
    key_step = jnp.dot(jnp.transpose(fitness[:, None] * fac_a), fac_b, precision=lax.Precision.HIGHEST) * scale
    value_step = jnp.dot(jnp.transpose(fitness[:, None] * fac_c), fac_d, precision=lax.Precision.HIGHEST) * scale
    return outputs, key_step, value_step
```

```python
import jax
import jax.numpy as jnp
from jax import lax
from jax.sharding import Mesh
from jax.sharding import PartitionSpec as P

D = 4096
FF = 16384
BATCH = 64
MEMBERS = 128
Y = ("y_hi", "y_lo")
HIGH = lax.Precision.HIGHEST


def swap(x):
    return lax.ppermute(x, "core", [(0, 1), (1, 0)])


def to_all(x, axis, n):
    return lax.all_to_all(jnp.broadcast_to(x[None], (n, *x.shape)), axis, 0, 0)


def one_hot(index, n):
    return (index[:, None] == lax.iota(jnp.int32, n)[None, :]).astype(jnp.float32)


def shards(inputs, mix, key_weight, value_weight, dim_bank, hidden_bank, member_picks, ranks):
    sigma_k = 0.5 / D**0.5
    sigma_v = 0.5 / FF**0.5
    bank = dim_bank.shape[0]
    tok, feat = inputs.shape
    hid = key_weight.shape[1]
    half = hid // 2
    own = tok // BATCH
    core = lax.axis_index("core")
    y_hi = lax.axis_index("y_hi")
    z = lax.axis_index("z")

    key_rows = key_weight.T
    key_mine = lax.dynamic_slice_in_dim(key_rows, core * half, half, 0)
    key_else = lax.dynamic_slice_in_dim(key_rows, (1 - core) * half, half, 0)
    value_mine = lax.dynamic_slice_in_dim(value_weight, core * half, half, 0)
    value_else = lax.dynamic_slice_in_dim(value_weight, (1 - core) * half, half, 0)
    got = swap(jnp.concatenate([key_else, value_else], axis=1))
    packed = jnp.concatenate([key_mine, got[:, :feat], value_mine, got[:, feat:]], axis=1)
    weights = lax.all_gather(packed, "z", axis=0, tiled=True)

    values = inputs.astype(jnp.float32).reshape(own, BATCH, feat)
    previous = jnp.concatenate([jnp.zeros((own, 1, feat), jnp.float32), values[:, :-1, :]], axis=1)
    shifted = (values + (previous - values) * mix).reshape(tok, feat).astype(jnp.bfloat16)
    info = jnp.concatenate([member_picks, ranks[:, None]], axis=1).astype(jnp.bfloat16)
    info = jnp.pad(info, ((0, 16 - own), (0, feat - info.shape[1])))
    group = to_all(jnp.concatenate([shifted, info], axis=0), Y, 8)
    mine = group[:, :tok].reshape(8 * tok, feat)
    tokens = jnp.concatenate([mine, swap(mine)], axis=1)
    members = 8 * own
    info = group[:, tok : tok + own, :128].reshape(members, 128)
    everyone = to_all(info, "z", 8).reshape(8 * members, 128)[:, :5].astype(jnp.int32)
    info = info[:, :4].astype(jnp.int32)

    banks = jnp.concatenate([dim_bank, swap(dim_bank)], axis=1)
    hidden = hidden_bank.reshape(bank, 8, 2, 2, half)
    hidden = lax.dynamic_index_in_dim(hidden, y_hi, 2, keepdims=False)
    hidden_own = lax.dynamic_index_in_dim(hidden, z, 1, keepdims=False).reshape(bank, hid)
    hidden = lax.dynamic_index_in_dim(hidden, core, 2, keepdims=False).reshape(bank, 8 * half)
    fac_a = jnp.dot(one_hot(info[:, 0], bank), banks, precision=HIGH)
    fac_b = jnp.dot(one_hot(info[:, 1], bank), hidden, precision=HIGH)
    fac_c = jnp.dot(one_hot(info[:, 2], bank), hidden, precision=HIGH)
    fac_d = jnp.dot(one_hot(info[:, 3], bank), banks, precision=HIGH)

    inner = jnp.sum(
        tokens.astype(jnp.float32).reshape(members, BATCH, -1) * fac_a[:, None, :], axis=-1
    )
    key_all = weights[:, : 2 * feat]
    product = lax.dot_general(
        tokens, key_all, (((1,), (1,)), ((), ())), preferred_element_type=jnp.float32
    )
    part = product.reshape(members, BATCH, -1) + sigma_k * inner[:, :, None] * fac_b[:, None, :]
    part = part.reshape(4, 2 * tok, -1).astype(jnp.bfloat16)
    parts = lax.all_to_all(part, "x", 0, 0)
    key_pre = jnp.sum(parts.astype(jnp.float32), axis=0)
    keys = (jnp.maximum(key_pre, 0.0) ** 2).astype(jnp.bfloat16)
    keys = to_all(keys, "x", 4).reshape(8 * tok, -1)

    inner_c = jnp.sum(
        keys.astype(jnp.float32).reshape(members, BATCH, -1) * fac_c[:, None, :], axis=-1
    )
    base = jnp.dot(keys, weights[:, 2 * feat :], preferred_element_type=jnp.float32)
    result = base.reshape(members, BATCH, -1) + sigma_v * inner_c[:, :, None] * fac_d[:, None, :]
    result = result.reshape(8 * tok, -1)
    rest = swap(result[:, feat:].astype(jnp.bfloat16))
    result = (result[:, :feat] + rest.astype(jnp.float32)).astype(jnp.bfloat16)
    pieces = lax.all_to_all(result.reshape(8, tok, feat), Y, 0, 0)
    outputs = jnp.sum(pieces.astype(jnp.float32), axis=0).astype(jnp.bfloat16)

    fitness = 2.0 * everyone[:, 4].astype(jnp.float32) / (MEMBERS - 1) - 1.0
    fitness = fitness * (1.0 / MEMBERS**0.5)
    pick = [one_hot(everyone[:, i], bank) for i in range(4)]
    pair_k = jnp.dot((fitness[:, None] * pick[0]).T, pick[1], precision=HIGH)
    pair_v = jnp.dot((fitness[:, None] * pick[2]).T, pick[3], precision=HIGH)
    key_step = jnp.dot(dim_bank.T, jnp.dot(pair_k, hidden_own, precision=HIGH), precision=HIGH)
    value_step = jnp.dot(hidden_own.T, jnp.dot(pair_v, dim_bank, precision=HIGH), precision=HIGH)
    return outputs, key_step, value_step


def solution(mesh):
    fine = Mesh(mesh.devices.reshape(8, 2, 4, 4, 2), ("z", "y_hi", "y_lo", "x", "core"))
    pop, row, col = ("z", "y_hi"), ("y_lo",), ("x", "core")
    in_specs = (
        P(pop + row, col),
        P(col),
        P(col, row + pop),
        P(row + pop, col),
        P(None, col),
        P(None, row),
        P(pop + row, None),
        P(pop + row),
    )
    out_specs = (P(pop + row, col), P(col, row + pop), P(row + pop, col))
    return jax.shard_map(shards, mesh=fine, in_specs=in_specs, out_specs=out_specs, check_vma=False)
```

```python
import functools

import jax
import jax.numpy as jnp
from jax import lax
from jax.experimental import pallas as pl
from jax.experimental.pallas import tpu as pltpu
from jax.sharding import Mesh
from jax.sharding import PartitionSpec as P

D = 4096
FF = 16384
BATCH = 64
MEMBERS = 128
NY = 8
NX = 4
Y = ("y_hi", "y_lo")
HIGH = lax.Precision.HIGHEST
SIGMA_K = 0.5 / D**0.5
SIGMA_V = 0.5 / FF**0.5
VMEM = pl.BlockSpec(memory_space=pltpu.VMEM)
SMEM = pl.BlockSpec(memory_space=pltpu.SMEM)


def swap(x):
    return lax.ppermute(x, "core", [(0, 1), (1, 0)])


def turn(x, by):
    return lax.ppermute(x, "x", [(i, (i + by) % NX) for i in range(NX)])


def to_all(x, axis, n):
    return lax.all_to_all(jnp.broadcast_to(x[None], (n, *x.shape)), axis, 0, 0)


def one_hot(index, n):
    return (index[:, None] == lax.iota(jnp.int32, n)[None, :]).astype(jnp.float32)


def key_kernel(chunk, x_ref, info_ref, mine_ref, got_ref, w_ref, bank_ref, hid_ref, *rest):
    outs, rows_ref = rest[:NX], rest[NX]
    feat = mine_ref.shape[2]
    inner, picks = [], []
    for s in range(NX):
        for k in range(NY // NX):
            y = lax.rem(x_ref[0] + s, NX) * (NY // NX) + k
            at = (s * (NY // NX) + k) * BATCH
            rows_ref[at : at + BATCH, :feat] = mine_ref[y, chunk * BATCH : (chunk + 1) * BATCH, :]
            rows_ref[at : at + BATCH, feat:] = got_ref[y, chunk * BATCH : (chunk + 1) * BATCH, :]
            member = y * 2 + chunk
            fac_a = bank_ref[pl.ds(info_ref[member, 0], 1), :]
            rows = rows_ref[at : at + BATCH, :].astype(jnp.float32)
            inner.append(SIGMA_K * jnp.sum(rows * fac_a, axis=1, keepdims=True))
            picks.append(info_ref[member, 1])
    rows = rows_ref[...]
    wide = 2 * w_ref.shape[2]
    for n in range(w_ref.shape[0] // 2):
        cols = slice(n * wide, (n + 1) * wide)
        w = jnp.concatenate([w_ref[2 * n], w_ref[2 * n + 1]], axis=1)
        acc = jnp.dot(rows, w, preferred_element_type=jnp.float32)
        for j in range(NY):
            fac_b = hid_ref[pl.ds(picks[j], 1), cols]
            term = acc[j * BATCH : (j + 1) * BATCH] + inner[j] * fac_b
            s, k = divmod(j, NY // NX)
            outs[s][k * BATCH : (k + 1) * BATCH, cols] = term.astype(jnp.bfloat16)


def out_kernel(chunk, half, x_ref, info_ref, *rest):
    keys, (v_ref, bank_ref, hid_ref, out_ref) = rest[:NX], rest[NX:]
    feat = out_ref.shape[2]
    cols = slice(half * feat, (half + 1) * feat)
    rows = jnp.concatenate([k[...] for k in keys], axis=0)
    v = v_ref[:, cols]
    acc = jnp.dot(rows, v, preferred_element_type=jnp.float32)
    for s in range(NX):
        for k in range(NY // NX):
            y = lax.rem(x_ref[0] + (NX - s), NX) * (NY // NX) + k
            member = y * 2 + chunk
            at = (s * (NY // NX) + k) * BATCH
            fac_c = hid_ref[pl.ds(info_ref[member, 2], 1), :]
            fac_d = bank_ref[pl.ds(info_ref[member, 3], 1), cols]
            own = keys[s][k * BATCH : (k + 1) * BATCH, :].astype(jnp.float32)
            inner = SIGMA_V * jnp.sum(own * fac_c, axis=1, keepdims=True)
            out_ref[y] = (acc[at : at + BATCH] + inner * fac_d).astype(out_ref.dtype)


def cost(rows, depth, cols):
    return pl.CostEstimate(
        flops=2 * rows * depth * cols,
        bytes_accessed=2 * (rows * depth + depth * cols + rows * cols),
        transcendentals=0,
    )


def key_part(chunk, x, info, mine, got, w, banks, hidden):
    rows, deep, wide = NY * BATCH, 2 * mine.shape[2], w.shape[0] * w.shape[2]
    out = jax.ShapeDtypeStruct((rows // NX, wide), jnp.bfloat16)
    return pl.pallas_call(
        functools.partial(key_kernel, chunk),
        out_shape=[out] * NX,
        in_specs=[SMEM, SMEM] + [VMEM] * 5,
        out_specs=[VMEM] * NX,
        scratch_shapes=[pltpu.VMEM((rows, deep), jnp.bfloat16)],
        compiler_params=pltpu.CompilerParams(vmem_limit_bytes=24 << 20),
        cost_estimate=cost(rows, deep, wide),
        name="key_part",
    )(x, info, mine, got, w, banks, hidden)


def out_part(chunk, half, dtype, x, info, keys, v, banks, hidden):
    rows, deep, feat = NY * BATCH, v.shape[0], v.shape[1] // 2
    return pl.pallas_call(
        functools.partial(out_kernel, chunk, half),
        out_shape=jax.ShapeDtypeStruct((NY, BATCH, feat), dtype),
        in_specs=[SMEM, SMEM] + [VMEM] * (NX + 3),
        out_specs=VMEM,
        compiler_params=pltpu.CompilerParams(vmem_limit_bytes=24 << 20),
        cost_estimate=cost(rows, deep, feat),
        name="out_part",
    )(x, info, *keys, v, banks, hidden)


def shards(inputs, mix, key_weight, value_weight, dim_bank, hidden_bank, member_picks, ranks):
    bank = dim_bank.shape[0]
    tok, feat = inputs.shape
    hid = key_weight.shape[1]
    half = hid // 2
    own = tok // BATCH
    core = lax.axis_index("core")
    y_hi = lax.axis_index("y_hi")
    z = lax.axis_index("z")
    x = lax.axis_index("x").reshape(1)

    def hidden_half(array, axis):
        return lax.dynamic_slice_in_dim(array, core * half, half, axis)

    key_pack = jnp.concatenate(
        [hidden_half(key_weight, 1), hidden_half(swap(key_weight), 1)], axis=0
    )
    key_all = lax.all_gather(key_pack, "z", axis=0)
    value_pack = jnp.concatenate(
        [hidden_half(value_weight, 0), hidden_half(swap(value_weight), 0)], axis=1
    )
    value_all = lax.all_gather(value_pack, "z", axis=0, tiled=True)

    values = inputs.astype(jnp.float32).reshape(own, BATCH, feat)
    previous = jnp.concatenate([jnp.zeros((own, 1, feat), jnp.float32), values[:, :-1, :]], axis=1)
    shifted = (values + (previous - values) * mix).reshape(tok, feat).astype(jnp.bfloat16)
    info = jnp.concatenate([member_picks, ranks[:, None]], axis=1).astype(jnp.bfloat16)
    info = jnp.pad(info, ((0, 16 - own), (0, feat - info.shape[1])))
    mine = to_all(jnp.concatenate([shifted, info], axis=0), Y, NY)
    got = swap(mine)
    members = NY * own
    info = mine[:, tok : tok + own, :128].reshape(members, 128)
    everyone = to_all(info, "z", 8).reshape(8 * members, 128)[:, :5].astype(jnp.int32)
    info = info[:, :4].astype(jnp.int32)

    banks = jnp.concatenate([dim_bank, swap(dim_bank)], axis=1)
    hidden = hidden_bank.reshape(bank, 8, 2, 2, half)
    hidden = lax.dynamic_index_in_dim(hidden, y_hi, 2, keepdims=False)
    hidden_own = lax.dynamic_index_in_dim(hidden, z, 1, keepdims=False).reshape(bank, hid)
    hidden = lax.dynamic_index_in_dim(hidden, core, 2, keepdims=False).reshape(bank, 8 * half)
    got, everyone = lax.optimization_barrier((got, everyone))

    parts = [key_part(c, x, info, mine, got, key_all, banks, hidden) for c in range(own)]
    sums = [[p[0]] + [turn(p[s], s) for s in (1, 3, 2)] for p in parts]
    keys = []
    for terms in sums:
        key_pre = sum(t.astype(jnp.float32) for t in terms)
        keys.append((jnp.maximum(key_pre, 0.0) ** 2).astype(jnp.bfloat16))
    keys = [[k] + [turn(k, s) for s in (1, 2, 3)] for k in keys]

    outputs = []
    for c in range(own):
        rest = out_part(c, 1, jnp.bfloat16, x, info, keys[c], value_all, banks, hidden)
        base = out_part(c, 0, jnp.float32, x, info, keys[c], value_all, banks, hidden)
        result = (base + swap(rest).astype(jnp.float32)).astype(jnp.bfloat16)
        pieces = lax.all_to_all(result, Y, 0, 0)
        outputs.append(jnp.sum(pieces.astype(jnp.float32), axis=0).astype(jnp.bfloat16))
    outputs = jnp.concatenate(outputs, axis=0)

    fitness = 2.0 * everyone[:, 4].astype(jnp.float32) / (MEMBERS - 1) - 1.0
    fitness = fitness * (1.0 / MEMBERS**0.5)
    pick = [one_hot(everyone[:, i], bank) for i in range(4)]
    pair_k = jnp.dot((fitness[:, None] * pick[0]).T, pick[1], precision=HIGH)
    pair_v = jnp.dot((fitness[:, None] * pick[2]).T, pick[3], precision=HIGH)
    key_step = jnp.dot(dim_bank.T, jnp.dot(pair_k, hidden_own, precision=HIGH), precision=HIGH)
    value_step = jnp.dot(hidden_own.T, jnp.dot(pair_v, dim_bank, precision=HIGH), precision=HIGH)
    return outputs, key_step, value_step


def solution(mesh):
    fine = Mesh(mesh.devices.reshape(8, 2, 4, 4, 2), ("z", "y_hi", "y_lo", "x", "core"))
    pop, row, col = ("z", "y_hi"), ("y_lo",), ("x", "core")
    in_specs = (
        P(pop + row, col),
        P(col),
        P(col, row + pop),
        P(row + pop, col),
        P(None, col),
        P(None, row),
        P(pop + row, None),
        P(pop + row),
    )
    out_specs = (P(pop + row, col), P(col, row + pop), P(row + pop, col))
    return jax.shard_map(shards, mesh=fine, in_specs=in_specs, out_specs=out_specs, check_vma=False)
```

```python
import functools

import jax
import jax.numpy as jnp
from jax import lax
from jax.experimental import pallas as pl
from jax.experimental.pallas import tpu as pltpu
from jax.sharding import Mesh
from jax.sharding import PartitionSpec as P

D = 4096
FF = 16384
BATCH = 64
MEMBERS = 128
NY = 8
NX = 4
INFO = 16
Y = ("y_hi", "y_lo")
HIGH = lax.Precision.HIGHEST
SIGMA_K = 0.5 / D**0.5
SIGMA_V = 0.5 / FF**0.5
VMEM = pl.BlockSpec(memory_space=pltpu.VMEM)
SMEM = pl.BlockSpec(memory_space=pltpu.SMEM)


def swap(x):
    return lax.ppermute(x, "core", [(0, 1), (1, 0)])


def one_hot(index, n):
    return (index[:, None] == lax.iota(jnp.int32, n)[None, :]).astype(jnp.float32)


def shift_kernel(copies, x_ref, mix_ref, info_ref, out_ref):
    tok = x_ref.shape[0]
    values = x_ref[...].astype(jnp.float32)
    first = lax.broadcasted_iota(jnp.int32, values.shape, 0) % BATCH == 0
    previous = jnp.where(first, 0.0, pltpu.roll(values, 1, 0))
    shifted = (values + (previous - values) * mix_ref[...]).astype(jnp.bfloat16)
    for i in range(copies):
        out_ref[i, :tok, :] = shifted
        out_ref[i, tok:, :] = info_ref[...]


def key_kernel(own, info_ref, mine_ref, got_ref, w_ref, bank_ref, hid_ref, out_ref, rows_ref):
    feat, tok = mine_ref.shape[2], own * BATCH
    inner = []
    for y in range(NY):
        rows_ref[y * tok : (y + 1) * tok, :feat] = mine_ref[y, :tok, :]
        rows_ref[y * tok : (y + 1) * tok, feat:] = got_ref[y, :tok, :]
    for m in range(NY * own):
        fac_a = bank_ref[pl.ds(info_ref[m, 0], 1), :]
        rows = rows_ref[m * BATCH : (m + 1) * BATCH, :].astype(jnp.float32)
        inner.append(SIGMA_K * jnp.sum(rows * fac_a, axis=1, keepdims=True))
    wide = 2 * w_ref.shape[2]
    block = out_ref.shape[1]
    for n in range(w_ref.shape[0] // 2):
        cols = slice(n * wide, (n + 1) * wide)
        w = jnp.concatenate([w_ref[2 * n], w_ref[2 * n + 1]], axis=1)
        acc = jnp.dot(rows_ref[...], w, preferred_element_type=jnp.float32)
        for m in range(NY * own):
            fac_b = hid_ref[pl.ds(info_ref[m, 1], 1), cols]
            term = acc[m * BATCH : (m + 1) * BATCH] + inner[m] * fac_b
            i, at = divmod(m * BATCH, block)
            out_ref[i, at : at + BATCH, cols] = term.astype(jnp.bfloat16)


def square_kernel(parts_ref, out_ref):
    block = 64
    for r in range(0, parts_ref.shape[1], block):
        total = sum(parts_ref[i, r : r + block, :].astype(jnp.float32) for i in range(NX))
        keys = (jnp.maximum(total, 0.0) ** 2).astype(jnp.bfloat16)
        for i in range(NX):
            out_ref[i, r : r + block, :] = keys


def out_kernel(half, info_ref, keys_ref, v_ref, bank_ref, hid_ref, out_ref):
    feat, half_hid = out_ref.shape[2], hid_ref.shape[1] // v_ref.shape[0]
    tok, block = out_ref.shape[1], keys_ref.shape[1]
    cols = slice(half * feat, (half + 1) * feat)
    v = jnp.concatenate([v_ref[i, :half_hid, cols] for i in range(v_ref.shape[0])], axis=0)
    for i in range(NX):
        acc = jnp.dot(keys_ref[i], v, preferred_element_type=jnp.float32)
        for j in range(block // BATCH):
            m = i * (block // BATCH) + j
            at = slice(j * BATCH, (j + 1) * BATCH)
            fac_c = hid_ref[pl.ds(info_ref[m, 2], 1), :]
            fac_d = bank_ref[pl.ds(info_ref[m, 3], 1), cols]
            inner = SIGMA_V * jnp.sum(
                keys_ref[i, at, :].astype(jnp.float32) * fac_c, axis=1, keepdims=True
            )
            y, row = divmod(m * BATCH, tok)
            out_ref[y, row : row + BATCH, :] = (acc[at] + inner * fac_d).astype(out_ref.dtype)


def cost(rows, depth, cols):
    return pl.CostEstimate(
        flops=2 * rows * depth * cols,
        bytes_accessed=2 * (rows * depth + depth * cols + rows * cols),
        transcendentals=0,
    )


def call(kernel, name, out, scratch, n_smem, estimate, *args):
    return pl.pallas_call(
        kernel,
        out_shape=jax.ShapeDtypeStruct(*out),
        in_specs=[SMEM] * n_smem + [VMEM] * (len(args) - n_smem),
        out_specs=VMEM,
        scratch_shapes=scratch,
        compiler_params=pltpu.CompilerParams(vmem_limit_bytes=24 << 20),
        cost_estimate=estimate,
        name=name,
    )(*args)


def out_part(half, dtype, info, keys, v, banks, hidden):
    rows, deep, feat = keys.shape[0] * keys.shape[1], keys.shape[2], v.shape[2] // 2
    out = (NY, rows // NY, feat), dtype
    kernel = functools.partial(out_kernel, half)
    return call(kernel, "out_part", out, [], 1, cost(rows, deep, feat), info, keys, v, banks, hidden)


def shards(inputs, mix, key_weight, value_weight, dim_bank, hidden_bank, member_picks, ranks):
    bank = dim_bank.shape[0]
    tok, feat = inputs.shape
    hid = key_weight.shape[1]
    half = hid // 2
    own = tok // BATCH
    core = lax.axis_index("core")
    y_hi = lax.axis_index("y_hi")
    z = lax.axis_index("z")

    info = jnp.concatenate([member_picks, ranks[:, None]], axis=1).astype(jnp.bfloat16)
    info = jnp.pad(info, ((0, INFO - own), (0, feat - info.shape[1])))
    shape = NY, tok + INFO, feat
    shifted = call(
        functools.partial(shift_kernel, NY), "shift", (shape, jnp.bfloat16), [], 0,
        cost(tok, 16, feat), inputs, mix[None], info,
    )
    mine = lax.all_to_all(shifted, Y, 0, 0)
    got = swap(mine)
    members = NY * own
    info = mine[:, tok : tok + own, :128].reshape(members, 128)
    ids = info[:, :4].astype(jnp.int32)

    def hidden_half(array, axis):
        return lax.dynamic_slice_in_dim(array, core * half, half, axis)

    key_pack = jnp.concatenate(
        [hidden_half(key_weight, 1), hidden_half(swap(key_weight), 1)], axis=0
    )
    key_all = lax.all_gather(key_pack, "z", axis=0)
    value_pack = jnp.concatenate(
        [hidden_half(value_weight, 0), hidden_half(swap(value_weight), 0)], axis=1
    )
    info = jnp.pad(info, ((0, INFO - members), (0, 2 * feat - 128)))
    value_all = lax.all_gather(jnp.concatenate([value_pack, info], axis=0), "z", axis=0)
    everyone = value_all[:, half : half + members, :5].reshape(8 * members, 5).astype(jnp.int32)

    banks = jnp.concatenate([dim_bank, swap(dim_bank)], axis=1)
    hidden = hidden_bank.reshape(bank, 8, 2, 2, half)
    hidden = lax.dynamic_index_in_dim(hidden, y_hi, 2, keepdims=False)
    hidden_own = lax.dynamic_index_in_dim(hidden, z, 1, keepdims=False).reshape(bank, hid)
    hidden = lax.dynamic_index_in_dim(hidden, core, 2, keepdims=False).reshape(bank, 8 * half)

    rows, deep, wide = NY * tok, 2 * feat, 8 * half
    blocks = (NX, rows // NX, wide), jnp.bfloat16
    part = call(
        functools.partial(key_kernel, own), "key_part", blocks,
        [pltpu.VMEM((rows, deep), jnp.bfloat16)], 1, cost(rows, deep, wide),
        ids, mine, got, key_all, banks, hidden,
    )
    parts = lax.all_to_all(part, "x", 0, 0)
    keys = call(square_kernel, "square", blocks, [], 0, cost(rows, 1, wide), parts)
    keys = lax.all_to_all(keys, "x", 0, 0)

    rest = out_part(1, jnp.bfloat16, ids, keys, value_all, banks, hidden)
    base = out_part(0, jnp.float32, ids, keys, value_all, banks, hidden)
    result = (base + swap(rest).astype(jnp.float32)).astype(jnp.bfloat16)
    pieces = lax.all_to_all(result, Y, 0, 0)
    outputs = jnp.sum(pieces.astype(jnp.float32), axis=0).astype(jnp.bfloat16)

    fitness = 2.0 * everyone[:, 4].astype(jnp.float32) / (MEMBERS - 1) - 1.0
    fitness = fitness * (1.0 / MEMBERS**0.5)
    pick = [one_hot(everyone[:, i], bank) for i in range(4)]
    pair_k = jnp.dot((fitness[:, None] * pick[0]).T, pick[1], precision=HIGH)
    pair_v = jnp.dot((fitness[:, None] * pick[2]).T, pick[3], precision=HIGH)
    key_step = jnp.dot(dim_bank.T, jnp.dot(pair_k, hidden_own, precision=HIGH), precision=HIGH)
    value_step = jnp.dot(hidden_own.T, jnp.dot(pair_v, dim_bank, precision=HIGH), precision=HIGH)
    return outputs, key_step, value_step


def solution(mesh):
    fine = Mesh(mesh.devices.reshape(8, 2, 4, 4, 2), ("z", "y_hi", "y_lo", "x", "core"))
    pop, row, col = ("z", "y_hi"), ("y_lo",), ("x", "core")
    in_specs = (
        P(pop + row, col),
        P(col),
        P(col, row + pop),
        P(row + pop, col),
        P(None, col),
        P(None, row),
        P(pop + row, None),
        P(pop + row),
    )
    out_specs = (P(pop + row, col), P(col, row + pop), P(row + pop, col))
    return jax.shard_map(shards, mesh=fine, in_specs=in_specs, out_specs=out_specs, check_vma=False)
```

```python
import functools

import jax
import jax.numpy as jnp
from jax import lax
from jax.experimental import pallas as pl
from jax.experimental.pallas import tpu as pltpu
from jax.sharding import Mesh
from jax.sharding import PartitionSpec as P

D = 4096
FF = 16384
BATCH = 64
MEMBERS = 128
NY, NQ = 8, 4
NX, NZ = 4, 8
INFO = 16
YQ = ("y_hi", "y_mid")
HIGH = lax.Precision.HIGHEST
SIGMA_K = 0.5 / D**0.5
SIGMA_V = 0.5 / FF**0.5
VMEM = pl.BlockSpec(memory_space=pltpu.VMEM)
HBM = pl.BlockSpec(memory_space=pltpu.HBM)
SMEM = pl.BlockSpec(memory_space=pltpu.SMEM)


def swap(x):
    return lax.ppermute(x, "core", [(0, 1), (1, 0)])


def exchange(x, second):
    pairs = []
    for i in range(NX):
        for core in range(2):
            to = i ^ 1 if core == second else NX - 1 - i
            pairs.append((2 * i + core, 2 * to + core))
    return lax.ppermute(x, ("x", "core"), pairs)


def beside(x):
    pairs = []
    for y in range(NY):
        for core in range(2):
            to = y ^ 1 if core == 0 else (y + 2 * (y % 2) - 1) % NY
            pairs.append((2 * y + core, 2 * to + core))
    return lax.ppermute(x, YQ + ("y_low", "core"), pairs)


def shift_kernel(copies, picks_hbm, ranks_hbm, x_hbm, mix_hbm, out_ref, picks_ref, ranks_ref, x_ref, mix_ref, sems):
    pairs = (x_hbm, x_ref), (mix_hbm, mix_ref), (picks_hbm, picks_ref), (ranks_hbm, ranks_ref)
    fetches = [pltpu.make_async_copy(src, dst, sems.at[i]) for i, (src, dst) in enumerate(pairs)]
    for fetch in fetches:
        fetch.start()
    for fetch in fetches:
        fetch.wait()
    tok, feat = x_ref.shape
    values = x_ref[...].astype(jnp.float32)
    first = lax.broadcasted_iota(jnp.int32, values.shape, 0) % BATCH == 0
    previous = jnp.where(first, 0.0, pltpu.roll(values, 1, 0))
    shifted = (values + (previous - values) * mix_ref[...]).astype(jnp.bfloat16)
    row = lax.broadcasted_iota(jnp.int32, (INFO, feat), 0)
    lane = lax.broadcasted_iota(jnp.int32, (INFO, feat), 1)
    info = jnp.zeros((INFO, feat), jnp.float32)
    for i in range(tok // BATCH):
        entries = [picks_ref[i, j] for j in range(4)] + [ranks_ref[i]]
        for j, entry in enumerate(entries):
            info = jnp.where((row == i) & (lane == j), entry.astype(jnp.float32), info)
    info = info.astype(jnp.bfloat16)
    for i in range(copies):
        out_ref[i, :tok, :] = shifted
        out_ref[i, tok:, :] = info


def hidden_kernel(at_ref, hid_hbm, out_ref, sems):
    apart, width = hid_hbm.shape[1] // NZ, out_ref.shape[1] // NZ
    fetches = []
    for i in range(NZ):
        start = pl.multiple_of(at_ref[0] + i * apart, width)
        src, dst = hid_hbm.at[:, pl.ds(start, width)], out_ref.at[:, pl.ds(i * width, width)]
        fetches.append(pltpu.make_async_copy(src, dst, sems.at[i]))
        fetches[-1].start()
    for fetch in fetches:
        fetch.wait()


def key_kernel(order, order_ref, ids_ref, *refs):
    tokens, (w_ref, bank_ref, other_ref, hid_ref, *out_refs) = refs[:4], refs[4:]
    tok = tokens[0].shape[1] - INFO
    own = tok // BATCH
    blocks, inner, picks = [], [], []
    for i in order:
        u = order_ref[i]
        for s in range(2):
            for j in range(own):
                rows = [r[u, j * BATCH : (j + 1) * BATCH, :] for r in (tokens[s], tokens[2 + s])]
                m = (s * NX + u) * own + j
                fac_a = [r[pl.ds(ids_ref[m, 0], 1), :] for r in (bank_ref, other_ref)]
                dots = sum(r.astype(jnp.float32) * a for r, a in zip(rows, fac_a))
                inner.append(SIGMA_K * jnp.sum(dots, axis=1, keepdims=True))
                picks.append(ids_ref[m, 1])
                blocks.append(jnp.concatenate(rows, axis=1))
    rows = jnp.concatenate(blocks, axis=0)
    width, per = w_ref.shape[2], 2 * own
    for n in range(0, NZ, 2):
        cols = slice(n * width, (n + 2) * width)
        w = jnp.concatenate([w_ref[n], w_ref[n + 1]], axis=1)
        acc = jnp.dot(rows, w, preferred_element_type=jnp.float32)
        for k, (part, pick) in enumerate(zip(inner, picks)):
            term = acc[k * BATCH : (k + 1) * BATCH] + part * hid_ref[pl.ds(pick, 1), cols]
            i, at = divmod(k, per)
            out_refs[i][at * BATCH : (at + 1) * BATCH, cols] = term.astype(out_refs[i].dtype)


def add_kernel(kept_ref, came_ref, out_ref):
    out_ref[...] = (kept_ref[...] + came_ref[...].astype(jnp.float32)).astype(jnp.bfloat16)


def square_kernel(kept_ref, first_ref, second_ref, out_ref):
    total = kept_ref[...] + first_ref[...].astype(jnp.float32) + second_ref[...].astype(jnp.float32)
    out_ref[...] = (jnp.maximum(total, 0.0) ** 2).astype(jnp.bfloat16)


def out_kernel(half, order_ref, ids_ref, *refs):
    keys, (v_ref, bank_ref, hid_ref), rest = refs[:NX], refs[NX : NX + 3], refs[NX + 3 :]
    came, out_refs = rest[:-2], rest[-2:]
    feat, width = out_refs[0].shape[2], hid_ref.shape[1] // NZ
    tok = out_refs[0].shape[1]
    own, wide = tok // BATCH, 256
    inner, picks, places = [], [], []
    for i in range(NX):
        for s in range(2):
            for j in range(own):
                m = (s * NX + order_ref[i]) * own + j
                fac_c = hid_ref[pl.ds(ids_ref[m, 2], 1), :]
                at = s * tok + j * BATCH
                part = keys[i][at : at + BATCH, :].astype(jnp.float32)
                inner.append(SIGMA_V * jnp.sum(part * fac_c, axis=1, keepdims=True))
                picks.append(ids_ref[m, 3])
                places.append((s, order_ref[i], slice(j * BATCH, (j + 1) * BATCH)))
    rows = jnp.concatenate([k[...] for k in keys], axis=0)
    for n in range(feat // wide):
        cols = slice(n * wide, (n + 1) * wide)
        from_v = slice(half * feat + n * wide, half * feat + (n + 1) * wide)
        v = jnp.concatenate([v_ref[i, :width, from_v] for i in range(NZ)], axis=0)
        acc = jnp.dot(rows, v, preferred_element_type=jnp.float32)
        for k, (s, u, at) in enumerate(places):
            part = acc[k * BATCH : (k + 1) * BATCH] + inner[k] * bank_ref[pl.ds(picks[k], 1), cols]
            if came:
                part = part + came[s][u, at, cols].astype(jnp.float32)
            out_refs[s][u, at, cols] = part.astype(out_refs[s].dtype)


def step_kernel(at_ref, info_ref, bank_ref, hid_ref, key_ref, value_ref):
    info = info_ref[...].astype(jnp.float32)
    fitness = 2.0 * info[:, 4:5] / (MEMBERS - 1) - 1.0
    fitness = fitness * (1.0 / MEMBERS**0.5)
    lane = lax.broadcasted_iota(jnp.int32, (info.shape[0], bank_ref.shape[0]), 1).astype(jnp.float32)
    pick = [(info[:, i : i + 1] == lane).astype(jnp.float32) for i in range(4)]
    hid = key_ref.shape[1]
    hidden = hid_ref[:, pl.ds(pl.multiple_of(at_ref[1], hid), hid)]

    def product(a, b, contract):
        dims = ((contract,), (0,)), ((), ())
        return lax.dot_general(a, b, dims, precision=HIGH, preferred_element_type=jnp.float32)

    pair_k = product(fitness * pick[0], pick[1], 0)
    pair_v = product(fitness * pick[2], pick[3], 0)
    key_ref[...] = product(bank_ref[...], product(pair_k, hidden, 1), 0)
    value_ref[...] = product(hidden, product(pair_v, bank_ref[...], 1), 0)


def cost(rows, depth, cols):
    return pl.CostEstimate(
        flops=2 * rows * depth * cols,
        bytes_accessed=2 * (rows * depth + depth * cols + rows * cols),
        transcendentals=0,
    )


def call(kernel, name, outs, specs, estimate, args, scratch=()):
    args = [pltpu.with_memory_space_constraint(a, pltpu.HBM) if s is HBM else a for a, s in zip(args, specs)]
    return pl.pallas_call(
        kernel,
        out_shape=[jax.ShapeDtypeStruct(*out) for out in outs],
        in_specs=specs,
        out_specs=[VMEM] * len(outs),
        scratch_shapes=scratch,
        compiler_params=pltpu.CompilerParams(vmem_limit_bytes=16 << 20),
        cost_estimate=estimate,
        name=name,
    )(*args)


def shards(inputs, mix, key_weight, value_weight, dim_bank, hidden_bank, member_picks, ranks):
    tok, feat = inputs.shape
    hid = key_weight.shape[1]
    half = hid // 2
    own = tok // BATCH
    core, x, z = lax.axis_index("core"), lax.axis_index("x"), lax.axis_index("z")
    block = (z * 2 + lax.axis_index("y_hi")) * hid
    at = jnp.stack([lax.axis_index("y_hi") * hid + core * half, block]).astype(jnp.int32)

    key_other, value_other, bank_other = swap(key_weight), swap(value_weight), swap(dim_bank)
    scratch = [
        pltpu.SMEM(member_picks.shape, jnp.int32), pltpu.SMEM(ranks.shape, jnp.int32),
        pltpu.VMEM(inputs.shape, jnp.bfloat16), pltpu.VMEM((1, feat), jnp.float32),
        pltpu.SemaphoreType.DMA((4,)),
    ]
    shifted = call(
        functools.partial(shift_kernel, NQ), "shift", [((NQ, tok + INFO, feat), jnp.bfloat16)],
        [HBM] * 4, cost(tok, 16, feat), (member_picks, ranks, inputs, mix[None]), scratch,
    )[0]
    same = lax.all_to_all(shifted, YQ, 0, 0)
    other = beside(same)
    tokens = same, other, swap(same), swap(other)
    members = NY * own
    info = jnp.stack([t[:, tok : tok + own, :128] for t in (same, other)]).reshape(members, 128)
    ids = info[:, :4].astype(jnp.int32)

    def hidden_half(array, axis):
        return lax.dynamic_slice_in_dim(array, core * half, half, axis)

    key_pack = jnp.concatenate([hidden_half(key_weight, 1), hidden_half(key_other, 1)], axis=0)
    key_all = lax.all_gather(key_pack, "z", axis=0)
    value_other, bank_other = lax.optimization_barrier((value_other, bank_other))
    value_pack = jnp.concatenate([hidden_half(value_weight, 0), hidden_half(value_other, 0)], axis=1)
    info = jnp.pad(info, ((0, INFO - members), (0, 2 * feat - 128)))
    value_all = lax.all_gather(jnp.concatenate([value_pack, info], axis=0), "z", axis=0)
    everyone = value_all[:, half : half + members, :128].reshape(NZ * members, 128)

    lo, hi = lax.rem(x, 2), x // 2
    f, g = jnp.where(core == 0, lax.rem(lo + hi, 2), hi), jnp.where(core == 0, hi, lo)
    turned = jnp.where(core == 0, 1 - g, g)
    order = [2 * f + g, 2 * f + 1 - g, 2 * (1 - f) + turned, 2 * (1 - f) + 1 - turned]
    order = jnp.stack(order).astype(jnp.int32)
    deep, wide, quarter = 2 * feat, NZ * half, NY * tok // NX
    low, high = ((quarter, wide), jnp.bfloat16), ((quarter, wide), jnp.float32)
    hidden = call(
        hidden_kernel, "hidden", [((hidden_bank.shape[0], wide), jnp.float32)], [SMEM, HBM],
        cost(hidden_bank.shape[0], 1, wide), (at, hidden_bank), [pltpu.SemaphoreType.DMA((NZ,))],
    )[0]

    def key_part(which, outs):
        return call(
            functools.partial(key_kernel, which), "key_part", outs,
            [SMEM] * 2 + [VMEM] * 8, cost(len(which) * quarter, deep, wide),
            (order, ids, *tokens, key_all, dim_bank, bank_other, hidden),
        )

    def local(kernel, name, *args):
        return call(kernel, name, [low], [VMEM] * len(args), cost(quarter, 4, wide), args)[0]

    came_first = exchange(key_part((2,), [low])[0], 0)
    came_second = exchange(key_part((3,), [low])[0], 0)
    following, kept = key_part((1, 0), [high, high])
    came_next = exchange(local(add_kernel, "add", following, came_first), 1)
    key_own = local(square_kernel, "square", kept, came_second, came_next)

    key_next = exchange(key_own, 1)
    key_own, key_next = lax.optimization_barrier((key_own, key_next))
    key_second = exchange(key_own, 0)
    key_first = exchange(key_next, 0)
    keys = key_own, key_next, key_first, key_second

    def out_part(half, bank, kept, *came):
        out = NQ, tok, feat
        return call(
            functools.partial(out_kernel, half), "out_part", [(out, kept), (out, jnp.bfloat16)],
            [SMEM] * 2 + [VMEM] * (NX + 3 + len(came)), cost(NY * tok, wide, feat),
            (order, ids, *keys, value_all, bank, hidden, *came),
        )

    came = [swap(rest) for rest in out_part(1, bank_other, jnp.bfloat16)]
    same, other = out_part(0, dim_bank, jnp.float32, *came)
    pieces = (same + beside(other).astype(jnp.float32)).astype(jnp.bfloat16)
    pieces, everyone = lax.optimization_barrier((pieces, everyone))
    pieces = lax.all_to_all(pieces, YQ, 0, 0)
    outputs = jnp.sum(pieces.astype(jnp.float32), axis=0).astype(jnp.bfloat16)
    key_step, value_step = call(
        step_kernel, "steps", [(key_weight.shape, jnp.float32), (value_weight.shape, jnp.float32)],
        [SMEM] + [VMEM] * 3, cost(hid, 512, feat), (at, everyone, dim_bank, hidden_bank),
    )
    return outputs, key_step, value_step


def solution(mesh):
    axes = ("z", "y_hi", "y_mid", "y_low", "x", "core")
    fine = Mesh(mesh.devices.reshape(8, 2, 2, 2, 4, 2), axes)
    pop, row, col = ("z", "y_hi"), ("y_mid", "y_low"), ("x", "core")
    in_specs = (
        P(pop + row, col),
        P(col),
        P(col, row + pop),
        P(row + pop, col),
        P(None, col),
        P(None, row),
        P(pop + row, None),
        P(pop + row),
    )
    out_specs = (P(pop + row, col), P(col, row + pop), P(row + pop, col))
    return jax.shard_map(shards, mesh=fine, in_specs=in_specs, out_specs=out_specs, check_vma=False)
```

```python
import functools

import jax
import jax.numpy as jnp
from jax import lax
from jax.experimental import pallas as pl
from jax.experimental.pallas import tpu as pltpu
from jax.sharding import Mesh
from jax.sharding import PartitionSpec as P

D = 4096
FF = 16384
BATCH = 64
MEMBERS = 128
NY, NQ = 8, 4
NX, NZ = 4, 8
INFO = 16
YQ = ("y_hi", "y_mid")
HIGH = lax.Precision.HIGHEST
SIGMA_K = 0.5 / D**0.5
SIGMA_V = 0.5 / FF**0.5
VMEM = pl.BlockSpec(memory_space=pltpu.VMEM)
HBM = pl.BlockSpec(memory_space=pltpu.HBM)
ANY = pl.BlockSpec(memory_space=pl.ANY)
SMEM = pl.BlockSpec(memory_space=pltpu.SMEM)


def swap(x):
    return lax.ppermute(x, "core", [(0, 1), (1, 0)])


def exchange(x, second):
    pairs = []
    for i in range(NX):
        for core in range(2):
            to = i ^ 1 if core == second else NX - 1 - i
            pairs.append((2 * i + core, 2 * to + core))
    return lax.ppermute(x, ("x", "core"), pairs)


def beside(x):
    pairs = []
    for y in range(NY):
        for core in range(2):
            to = y ^ 1 if core == 0 else (y + 2 * (y % 2) - 1) % NY
            pairs.append((2 * y + core, 2 * to + core))
    return lax.ppermute(x, YQ + ("y_low", "core"), pairs)


def shift_kernel(copies, picks_hbm, ranks_hbm, x_hbm, mix_hbm, out_ref, picks_ref, ranks_ref, x_ref, mix_ref, sems):
    pairs = (x_hbm, x_ref), (mix_hbm, mix_ref), (picks_hbm, picks_ref), (ranks_hbm, ranks_ref)
    fetches = [pltpu.make_async_copy(src, dst, sems.at[i]) for i, (src, dst) in enumerate(pairs)]
    for fetch in fetches:
        fetch.start()
    for fetch in fetches:
        fetch.wait()
    tok, feat = x_ref.shape
    values = x_ref[...].astype(jnp.float32)
    first = lax.broadcasted_iota(jnp.int32, values.shape, 0) % BATCH == 0
    previous = jnp.where(first, 0.0, pltpu.roll(values, 1, 0))
    shifted = (values + (previous - values) * mix_ref[...]).astype(jnp.bfloat16)
    row = lax.broadcasted_iota(jnp.int32, (INFO, feat), 0)
    lane = lax.broadcasted_iota(jnp.int32, (INFO, feat), 1)
    info = jnp.zeros((INFO, feat), jnp.float32)
    for i in range(tok // BATCH):
        entries = [picks_ref[i, j] for j in range(4)] + [ranks_ref[i]]
        for j, entry in enumerate(entries):
            info = jnp.where((row == i) & (lane == j), entry.astype(jnp.float32), info)
    info = info.astype(jnp.bfloat16)
    for i in range(copies):
        out_ref[i, :tok, :] = shifted
        out_ref[i, tok:, :] = info


def hidden_kernel(at_ref, hid_hbm, out_ref, sems):
    apart, width = hid_hbm.shape[1] // NZ, out_ref.shape[1] // NZ
    fetches = []
    for i in range(NZ):
        start = pl.multiple_of(at_ref[0] + i * apart, width)
        src, dst = hid_hbm.at[:, pl.ds(start, width)], out_ref.at[:, pl.ds(i * width, width)]
        fetches.append(pltpu.make_async_copy(src, dst, sems.at[i]))
        fetches[-1].start()
    for fetch in fetches:
        fetch.wait()


def key_kernel(order, order_ref, ids_ref, *refs):
    tokens, (w_ref, bank_ref, other_ref, hid_ref, *out_refs) = refs[:4], refs[4:]
    tok = tokens[0].shape[1] - INFO
    own = tok // BATCH
    blocks, inner, picks = [], [], []
    for i in order:
        u = order_ref[i]
        for s in range(2):
            for j in range(own):
                rows = [r[u, j * BATCH : (j + 1) * BATCH, :] for r in (tokens[s], tokens[2 + s])]
                m = (s * NX + u) * own + j
                fac_a = [r[pl.ds(ids_ref[m, 0], 1), :] for r in (bank_ref, other_ref)]
                dots = sum(r.astype(jnp.float32) * a for r, a in zip(rows, fac_a))
                inner.append(SIGMA_K * jnp.sum(dots, axis=1, keepdims=True))
                picks.append(ids_ref[m, 1])
                blocks.append(jnp.concatenate(rows, axis=1))
    rows = jnp.concatenate(blocks, axis=0)
    width, per = w_ref.shape[2], 2 * own
    for n in range(0, NZ, 2):
        cols = slice(n * width, (n + 2) * width)
        w = jnp.concatenate([w_ref[n], w_ref[n + 1]], axis=1)
        acc = jnp.dot(rows, w, preferred_element_type=jnp.float32)
        for k, (part, pick) in enumerate(zip(inner, picks)):
            term = acc[k * BATCH : (k + 1) * BATCH] + part * hid_ref[pl.ds(pick, 1), cols]
            i, at = divmod(k, per)
            out_refs[i][at * BATCH : (at + 1) * BATCH, cols] = term.astype(out_refs[i].dtype)


def add_kernel(kept_ref, came_ref, out_ref):
    out_ref[...] = (kept_ref[...] + came_ref[...].astype(jnp.float32)).astype(jnp.bfloat16)


def square_kernel(kept_ref, first_ref, second_ref, out_ref):
    total = kept_ref[...] + first_ref[...].astype(jnp.float32) + second_ref[...].astype(jnp.float32)
    out_ref[...] = (jnp.maximum(total, 0.0) ** 2).astype(jnp.bfloat16)


def out_kernel(half, order, order_ref, ids_ref, *refs):
    keys, (v_ref, bank_ref, hid_ref, *_, out_ref) = refs[: len(order)], refs[len(order) :]
    feat, width = out_ref.shape[3], hid_ref.shape[1] // NZ
    tok = out_ref.shape[2]
    own, wide = tok // BATCH, 256
    inner, picks, places = [], [], []
    for i, o in enumerate(order):
        for s in range(2):
            for j in range(own):
                m = (s * NX + order_ref[o]) * own + j
                fac_c = hid_ref[pl.ds(ids_ref[m, 2], 1), :]
                at = s * tok + j * BATCH
                part = keys[i][at : at + BATCH, :].astype(jnp.float32)
                inner.append(SIGMA_V * jnp.sum(part * fac_c, axis=1, keepdims=True))
                picks.append(ids_ref[m, 3])
                places.append((i, s, slice(j * BATCH, (j + 1) * BATCH)))
    rows = jnp.concatenate([k[...] for k in keys], axis=0)
    for n in range(feat // wide):
        cols = slice(n * wide, (n + 1) * wide)
        from_v = slice(half * feat + n * wide, half * feat + (n + 1) * wide)
        v = jnp.concatenate([v_ref[i, :width, from_v] for i in range(NZ)], axis=0)
        acc = jnp.dot(rows, v, preferred_element_type=jnp.float32)
        for k, (i, s, at) in enumerate(places):
            part = acc[k * BATCH : (k + 1) * BATCH] + inner[k] * bank_ref[pl.ds(picks[k], 1), cols]
            out_ref[i, s, at, cols] = part.astype(out_ref.dtype)


def place_kernel(orders, order_ref, at_ref, *refs):
    parts, out_ref = refs[:-1], refs[-1]
    twins = (0, 2, 1)
    for order, mine_ref, came_ref in zip(orders, parts[::2], parts[1::2]):
        for i, o in enumerate(order):
            for s in range(2):
                total = mine_ref[i, s] + came_ref[twins[i], s].astype(jnp.float32)
                out_ref[2 * order_ref[o] + lax.rem(at_ref[2] + s, 2)] = total.astype(jnp.bfloat16)


def step_kernel(at_ref, info_ref, bank_ref, hid_ref, key_ref, value_ref):
    info = info_ref[...].astype(jnp.float32)
    fitness = 2.0 * info[:, 4:5] / (MEMBERS - 1) - 1.0
    fitness = fitness * (1.0 / MEMBERS**0.5)
    lane = lax.broadcasted_iota(jnp.int32, (info.shape[0], bank_ref.shape[0]), 1).astype(jnp.float32)
    pick = [(info[:, i : i + 1] == lane).astype(jnp.float32) for i in range(4)]
    hid = key_ref.shape[1]
    hidden = hid_ref[:, pl.ds(pl.multiple_of(at_ref[1], hid), hid)]

    def product(a, b, contract):
        dims = ((contract,), (0,)), ((), ())
        return lax.dot_general(a, b, dims, precision=HIGH, preferred_element_type=jnp.float32)

    pair_k = product(fitness * pick[0], pick[1], 0)
    pair_v = product(fitness * pick[2], pick[3], 0)
    key_ref[...] = product(bank_ref[...], product(pair_k, hidden, 1), 0)
    value_ref[...] = product(hidden, product(pair_v, bank_ref[...], 1), 0)


def cost(rows, depth, cols):
    return pl.CostEstimate(
        flops=2 * rows * depth * cols,
        bytes_accessed=2 * (rows * depth + depth * cols + rows * cols),
        transcendentals=0,
    )


def call(kernel, name, outs, specs, estimate, args, scratch=()):
    args = [pltpu.with_memory_space_constraint(a, pltpu.HBM) if s is HBM else a for a, s in zip(args, specs)]
    return pl.pallas_call(
        kernel,
        out_shape=[jax.ShapeDtypeStruct(*out) for out in outs],
        in_specs=specs,
        out_specs=[VMEM] * len(outs),
        scratch_shapes=scratch,
        compiler_params=pltpu.CompilerParams(vmem_limit_bytes=16 << 20),
        cost_estimate=estimate,
        name=name,
    )(*args)


def shards(inputs, mix, key_weight, value_weight, dim_bank, hidden_bank, member_picks, ranks):
    tok, feat = inputs.shape
    hid = key_weight.shape[1]
    half = hid // 2
    own = tok // BATCH
    core, x, z = lax.axis_index("core"), lax.axis_index("x"), lax.axis_index("z")
    block = (z * 2 + lax.axis_index("y_hi")) * hid
    at = [lax.axis_index("y_hi") * hid + core * half, block, lax.axis_index("y_low")]
    at = jnp.stack(at).astype(jnp.int32)

    key_other, value_other, bank_other = swap(key_weight), swap(value_weight), swap(dim_bank)
    scratch = [
        pltpu.SMEM(member_picks.shape, jnp.int32), pltpu.SMEM(ranks.shape, jnp.int32),
        pltpu.VMEM(inputs.shape, jnp.bfloat16), pltpu.VMEM((1, feat), jnp.float32),
        pltpu.SemaphoreType.DMA((4,)),
    ]
    shifted = call(
        functools.partial(shift_kernel, NQ), "shift", [((NQ, tok + INFO, feat), jnp.bfloat16)],
        [HBM] * 4, cost(tok, 16, feat), (member_picks, ranks, inputs, mix[None]), scratch,
    )[0]
    same = lax.all_to_all(shifted, YQ, 0, 0)
    other = beside(same)
    tokens = same, other, swap(same), swap(other)
    members = NY * own
    info = jnp.stack([t[:, tok : tok + own, :128] for t in (same, other)]).reshape(members, 128)
    ids = info[:, :4].astype(jnp.int32)

    def hidden_half(array, axis):
        return lax.dynamic_slice_in_dim(array, core * half, half, axis)

    key_pack = jnp.concatenate([hidden_half(key_weight, 1), hidden_half(key_other, 1)], axis=0)
    key_all = lax.all_gather(key_pack, "z", axis=0)
    value_other, bank_other = lax.optimization_barrier((value_other, bank_other))
    value_pack = jnp.concatenate([hidden_half(value_weight, 0), hidden_half(value_other, 0)], axis=1)
    info = jnp.pad(info, ((0, INFO - members), (0, 2 * feat - 128)))
    value_all = lax.all_gather(jnp.concatenate([value_pack, info], axis=0), "z", axis=0)
    everyone = value_all[:, half : half + members, :128].reshape(NZ * members, 128)

    lo, hi = lax.rem(x, 2), x // 2
    f, g = jnp.where(core == 0, lax.rem(lo + hi, 2), hi), jnp.where(core == 0, hi, lo)
    turned = jnp.where(core == 0, 1 - g, g)
    order = []
    for upper, lower in ((f, g), (f, 1 - g), (1 - f, turned), (1 - f, 1 - turned)):
        order.append(jnp.where(core == 0, 2 * lower + lax.rem(upper + lower, 2), 2 * upper + lower))
    order = jnp.stack(order).astype(jnp.int32)
    deep, wide, quarter = 2 * feat, NZ * half, NY * tok // NX
    low, high = ((quarter, wide), jnp.bfloat16), ((quarter, wide), jnp.float32)
    hidden = call(
        hidden_kernel, "hidden", [((hidden_bank.shape[0], wide), jnp.float32)], [SMEM, HBM],
        cost(hidden_bank.shape[0], 1, wide), (at, hidden_bank), [pltpu.SemaphoreType.DMA((NZ,))],
    )[0]

    def key_part(which, outs):
        return call(
            functools.partial(key_kernel, which), "key_part", outs,
            [SMEM] * 2 + [VMEM] * 8, cost(len(which) * quarter, deep, wide),
            (order, ids, *tokens, key_all, dim_bank, bank_other, hidden),
        )

    def local(kernel, name, *args):
        return call(kernel, name, [low], [VMEM] * len(args), cost(quarter, 4, wide), args)[0]

    came_first = exchange(key_part((2,), [low])[0], 0)
    came_second = exchange(key_part((3,), [low])[0], 0)
    following, kept = key_part((1, 0), [high, high])
    came_next = exchange(local(add_kernel, "add", following, came_first), 1)
    key_own = local(square_kernel, "square", kept, came_second, came_next)

    before, after = NX - 1 - x, x + 1 - 2 * lo
    around = [x, jnp.where(core == 0, before, after), jnp.where(core == 0, after, before), lax.rem(x + 2, NX)]
    around = jnp.stack(around).astype(jnp.int32)
    key_next = exchange(key_own, 1)
    key_second = exchange(key_own, 0)
    keys = key_own, key_next, key_second, exchange(key_next, 0)

    def out_part(half, which, bank, kept, *after):
        out = len(which), 2, tok, feat
        return call(
            functools.partial(out_kernel, half, which), "out_part", [(out, kept)],
            [SMEM] * 2 + [VMEM] * (len(which) + 3) + [ANY] * len(after), cost(len(which) * quarter, wide, feat),
            (around, ids, *[keys[i] for i in which], value_all, bank, hidden, *after),
        )[0]

    sets = (0, 1, 2), (3,)
    parts = []
    for which in sets:
        came = swap(out_part(1, which, bank_other, jnp.bfloat16, *parts[:1]))
        parts += [out_part(0, which, dim_bank, jnp.float32), came]
    result = call(
        functools.partial(place_kernel, sets), "place", [((NY, tok, feat), jnp.bfloat16)],
        [SMEM] * 2 + [VMEM] * 4, cost(NY * tok, 1, feat), (around, at, *parts),
    )[0]
    result, everyone = lax.optimization_barrier((result, everyone))
    pieces = lax.all_to_all(result, YQ + ("y_low",), 0, 0)
    outputs = jnp.sum(pieces.astype(jnp.float32), axis=0).astype(jnp.bfloat16)
    key_step, value_step = call(
        step_kernel, "steps", [(key_weight.shape, jnp.float32), (value_weight.shape, jnp.float32)],
        [SMEM] + [VMEM] * 3, cost(hid, 512, feat), (at, everyone, dim_bank, hidden_bank),
    )
    return outputs, key_step, value_step


def solution(mesh):
    axes = ("z", "y_hi", "y_mid", "y_low", "x", "core")
    fine = Mesh(mesh.devices.reshape(8, 2, 2, 2, 4, 2), axes)
    pop, row, col = ("z", "y_hi"), ("y_mid", "y_low"), ("x", "core")
    in_specs = (
        P(pop + row, col),
        P(col),
        P(col, row + pop),
        P(row + pop, col),
        P(None, col),
        P(None, row),
        P(pop + row, None),
        P(pop + row),
    )
    out_specs = (P(pop + row, col), P(col, row + pop), P(row + pop, col))
    return jax.shard_map(shards, mesh=fine, in_specs=in_specs, out_specs=out_specs, check_vma=False)
```

```python
import functools

import jax
import jax.numpy as jnp
from jax import lax
from jax.experimental import pallas as pl
from jax.experimental.pallas import tpu as pltpu
from jax.sharding import Mesh
from jax.sharding import PartitionSpec as P

D = 4096
FF = 16384
BATCH = 64
MEMBERS = 128
NY, NQ = 8, 4
NX, NZ = 4, 8
INFO = 16
YQ = ("y_hi", "y_mid")
HIGH = lax.Precision.HIGHEST
SIGMA_K = 0.5 / D**0.5
SIGMA_V = 0.5 / FF**0.5
VMEM = pl.BlockSpec(memory_space=pltpu.VMEM)
HBM = pl.BlockSpec(memory_space=pltpu.HBM)
SMEM = pl.BlockSpec(memory_space=pltpu.SMEM)


def swap(x):
    return lax.ppermute(x, "core", [(0, 1), (1, 0)])


def exchange(x, second):
    pairs = []
    for i in range(NX):
        for core in range(2):
            to = i ^ 1 if core == second else NX - 1 - i
            pairs.append((2 * i + core, 2 * to + core))
    return lax.ppermute(x, ("x", "core"), pairs)


def beside(x):
    pairs = []
    for y in range(NY):
        for core in range(2):
            to = y ^ 1 if core == 0 else (y + 2 * (y % 2) - 1) % NY
            pairs.append((2 * y + core, 2 * to + core))
    return lax.ppermute(x, YQ + ("y_low", "core"), pairs)


def shift_kernel(copies, picks_hbm, ranks_hbm, x_hbm, mix_hbm, out_ref, picks_ref, ranks_ref, x_ref, mix_ref, sems):
    pairs = (x_hbm, x_ref), (mix_hbm, mix_ref), (picks_hbm, picks_ref), (ranks_hbm, ranks_ref)
    fetches = [pltpu.make_async_copy(src, dst, sems.at[i]) for i, (src, dst) in enumerate(pairs)]
    for fetch in fetches:
        fetch.start()
    for fetch in fetches:
        fetch.wait()
    tok, feat = x_ref.shape
    values = x_ref[...].astype(jnp.float32)
    first = lax.broadcasted_iota(jnp.int32, values.shape, 0) % BATCH == 0
    previous = jnp.where(first, 0.0, pltpu.roll(values, 1, 0))
    shifted = (values + (previous - values) * mix_ref[...]).astype(jnp.bfloat16)
    row = lax.broadcasted_iota(jnp.int32, (INFO, feat), 0)
    lane = lax.broadcasted_iota(jnp.int32, (INFO, feat), 1)
    info = jnp.zeros((INFO, feat), jnp.float32)
    for i in range(tok // BATCH):
        entries = [picks_ref[i, j] for j in range(4)] + [ranks_ref[i]]
        for j, entry in enumerate(entries):
            info = jnp.where((row == i) & (lane == j), entry.astype(jnp.float32), info)
    info = info.astype(jnp.bfloat16)
    for i in range(copies):
        out_ref[i, :tok, :] = shifted
        out_ref[i, tok:, :] = info


def hidden_kernel(at_ref, hid_hbm, out_ref, sems):
    apart, width = hid_hbm.shape[1] // NZ, out_ref.shape[1] // NZ
    fetches = []
    for i in range(NZ):
        start = pl.multiple_of(at_ref[0] + i * apart, width)
        src, dst = hid_hbm.at[:, pl.ds(start, width)], out_ref.at[:, pl.ds(i * width, width)]
        fetches.append(pltpu.make_async_copy(src, dst, sems.at[i]))
        fetches[-1].start()
    for fetch in fetches:
        fetch.wait()


def key_kernel(order, order_ref, ids_ref, *refs):
    tokens, (w_ref, bank_ref, other_ref, hid_ref, *out_refs) = refs[:4], refs[4:]
    tok = tokens[0].shape[1] - INFO
    own = tok // BATCH
    blocks, inner, picks = [], [], []
    for i in order:
        u = order_ref[i]
        for s in range(2):
            for j in range(own):
                rows = [r[u, j * BATCH : (j + 1) * BATCH, :] for r in (tokens[s], tokens[2 + s])]
                m = (s * NX + u) * own + j
                fac_a = [r[pl.ds(ids_ref[m, 0], 1), :] for r in (bank_ref, other_ref)]
                dots = sum(r.astype(jnp.float32) * a for r, a in zip(rows, fac_a))
                inner.append(SIGMA_K * jnp.sum(dots, axis=1, keepdims=True))
                picks.append(ids_ref[m, 1])
                blocks.append(jnp.concatenate(rows, axis=1))
    rows = jnp.concatenate(blocks, axis=0)
    width, per = w_ref.shape[2], 2 * own
    for n in range(0, NZ, 2):
        cols = slice(n * width, (n + 2) * width)
        w = jnp.concatenate([w_ref[n], w_ref[n + 1]], axis=1)
        acc = jnp.dot(rows, w, preferred_element_type=jnp.float32)
        for k, (part, pick) in enumerate(zip(inner, picks)):
            term = acc[k * BATCH : (k + 1) * BATCH] + part * hid_ref[pl.ds(pick, 1), cols]
            i, at = divmod(k, per)
            out_refs[i][at * BATCH : (at + 1) * BATCH, cols] = term.astype(out_refs[i].dtype)


def add_kernel(kept_ref, came_ref, out_ref):
    out_ref[...] = (kept_ref[...] + came_ref[...].astype(jnp.float32)).astype(jnp.bfloat16)


def square_kernel(mine_ref, came_ref, out_ref):
    total = mine_ref[...].astype(jnp.float32) + came_ref[...].astype(jnp.float32)
    out_ref[...] = (jnp.maximum(total, 0.0) ** 2).astype(jnp.bfloat16)


def out_kernel(half, order, order_ref, ids_ref, *refs):
    keys, (v_ref, bank_ref, hid_ref, *done, out_ref) = refs[: len(order)], refs[len(order) :]
    feat, width = out_ref.shape[3], hid_ref.shape[1] // NZ
    tok = out_ref.shape[2]
    own, wide = tok // BATCH, 256
    for ref in done:
        out_ref[: ref.shape[0]] = ref[...]
    inner, picks, places = [], [], []
    for i, o in enumerate(order):
        for s in range(2):
            for j in range(own):
                m = (s * NX + order_ref[o]) * own + j
                fac_c = hid_ref[pl.ds(ids_ref[m, 2], 1), :]
                at = s * tok + j * BATCH
                part = keys[i][at : at + BATCH, :].astype(jnp.float32)
                inner.append(SIGMA_V * jnp.sum(part * fac_c, axis=1, keepdims=True))
                picks.append(ids_ref[m, 3])
                places.append((out_ref.shape[0] - len(order) + i, s, slice(j * BATCH, (j + 1) * BATCH)))
    rows = jnp.concatenate([k[...] for k in keys], axis=0)
    for n in range(feat // wide):
        cols = slice(n * wide, (n + 1) * wide)
        from_v = slice(half * feat + n * wide, half * feat + (n + 1) * wide)
        v = jnp.concatenate([v_ref[i, :width, from_v] for i in range(NZ)], axis=0)
        acc = jnp.dot(rows, v, preferred_element_type=jnp.float32)
        for k, (i, s, at) in enumerate(places):
            part = acc[k * BATCH : (k + 1) * BATCH] + inner[k] * bank_ref[pl.ds(picks[k], 1), cols]
            out_ref[i, s, at, cols] = part.astype(out_ref.dtype)


def place_kernel(order_ref, at_ref, mine_ref, came_ref, out_ref):
    twins = (0, 2, 1, 3)
    for i in range(NX):
        for s in range(2):
            total = mine_ref[i, s] + came_ref[twins[i], s].astype(jnp.float32)
            out_ref[2 * order_ref[i] + lax.rem(at_ref[2] + s, 2)] = total.astype(jnp.bfloat16)


def step_kernel(at_ref, info_ref, bank_ref, hid_ref, key_ref, value_ref):
    info = info_ref[...].astype(jnp.float32)
    fitness = 2.0 * info[:, 4:5] / (MEMBERS - 1) - 1.0
    fitness = fitness * (1.0 / MEMBERS**0.5)
    lane = lax.broadcasted_iota(jnp.int32, (info.shape[0], bank_ref.shape[0]), 1).astype(jnp.float32)
    pick = [(info[:, i : i + 1] == lane).astype(jnp.float32) for i in range(4)]
    hid = key_ref.shape[1]
    hidden = hid_ref[:, pl.ds(pl.multiple_of(at_ref[1], hid), hid)]

    def product(a, b, contract):
        dims = ((contract,), (0,)), ((), ())
        return lax.dot_general(a, b, dims, precision=HIGH, preferred_element_type=jnp.float32)

    pair_k = product(fitness * pick[0], pick[1], 0)
    pair_v = product(fitness * pick[2], pick[3], 0)
    key_ref[...] = product(bank_ref[...], product(pair_k, hidden, 1), 0)
    value_ref[...] = product(hidden, product(pair_v, bank_ref[...], 1), 0)


def cost(rows, depth, cols):
    return pl.CostEstimate(
        flops=2 * rows * depth * cols,
        bytes_accessed=2 * (rows * depth + depth * cols + rows * cols),
        transcendentals=0,
    )


def call(kernel, name, outs, specs, estimate, args, scratch=()):
    args = [pltpu.with_memory_space_constraint(a, pltpu.HBM) if s is HBM else a for a, s in zip(args, specs)]
    return pl.pallas_call(
        kernel,
        out_shape=[jax.ShapeDtypeStruct(*out) for out in outs],
        in_specs=specs,
        out_specs=[VMEM] * len(outs),
        scratch_shapes=scratch,
        compiler_params=pltpu.CompilerParams(vmem_limit_bytes=16 << 20),
        cost_estimate=estimate,
        name=name,
    )(*args)


def shards(inputs, mix, key_weight, value_weight, dim_bank, hidden_bank, member_picks, ranks):
    tok, feat = inputs.shape
    hid = key_weight.shape[1]
    half = hid // 2
    own = tok // BATCH
    core, x, z = lax.axis_index("core"), lax.axis_index("x"), lax.axis_index("z")
    block = (z * 2 + lax.axis_index("y_hi")) * hid
    at = [lax.axis_index("y_hi") * hid + core * half, block, lax.axis_index("y_low")]
    at = jnp.stack(at).astype(jnp.int32)

    key_other, value_other, bank_other = swap(key_weight), swap(value_weight), swap(dim_bank)
    scratch = [
        pltpu.SMEM(member_picks.shape, jnp.int32), pltpu.SMEM(ranks.shape, jnp.int32),
        pltpu.VMEM(inputs.shape, jnp.bfloat16), pltpu.VMEM((1, feat), jnp.float32),
        pltpu.SemaphoreType.DMA((4,)),
    ]
    shifted = call(
        functools.partial(shift_kernel, NQ), "shift", [((NQ, tok + INFO, feat), jnp.bfloat16)],
        [HBM] * 4, cost(tok, 16, feat), (member_picks, ranks, inputs, mix[None]), scratch,
    )[0]
    same = lax.all_to_all(shifted, YQ, 0, 0)
    other = beside(same)
    tokens = same, other, swap(same), swap(other)
    members = NY * own
    info = jnp.stack([t[:, tok : tok + own, :128] for t in (same, other)]).reshape(members, 128)
    ids = info[:, :4].astype(jnp.int32)

    def hidden_half(array, axis):
        return lax.dynamic_slice_in_dim(array, core * half, half, axis)

    key_pack = jnp.concatenate([hidden_half(key_weight, 1), hidden_half(key_other, 1)], axis=0)
    key_all = lax.all_gather(key_pack, "z", axis=0)
    value_other, bank_other = lax.optimization_barrier((value_other, bank_other))
    value_pack = jnp.concatenate([hidden_half(value_weight, 0), hidden_half(value_other, 0)], axis=1)
    info = jnp.pad(info, ((0, INFO - members), (0, 2 * feat - 128)))
    value_all = lax.all_gather(jnp.concatenate([value_pack, info], axis=0), "z", axis=0)
    everyone = value_all[:, half : half + members, :128].reshape(NZ * members, 128)

    before, after = NX - 1 - x, x + 1 - 2 * lax.rem(x, 2)
    order = [x, jnp.where(core == 0, before, after), jnp.where(core == 0, after, before), lax.rem(x + 2, NX)]
    order = jnp.stack(order).astype(jnp.int32)
    deep, wide, quarter = 2 * feat, NZ * half, NY * tok // NX
    low, high = ((quarter, wide), jnp.bfloat16), ((quarter, wide), jnp.float32)
    hidden = call(
        hidden_kernel, "hidden", [((hidden_bank.shape[0], wide), jnp.float32)], [SMEM, HBM],
        cost(hidden_bank.shape[0], 1, wide), (at, hidden_bank), [pltpu.SemaphoreType.DMA((NZ,))],
    )[0]

    def key_part(which, outs):
        return call(
            functools.partial(key_kernel, which), "key_part", outs,
            [SMEM] * 2 + [VMEM] * 8, cost(len(which) * quarter, deep, wide),
            (order, ids, *tokens, key_all, dim_bank, bank_other, hidden),
        )

    def local(kernel, name, *args):
        return call(kernel, name, [low], [VMEM] * len(args), cost(quarter, 4, wide), args)[0]

    came_next = exchange(key_part((3,), [low])[0], 0)
    came_own = exchange(key_part((2,), [low])[0], 0)
    sum_next, sum_own = key_part((1, 0), [high, high])
    sum_next = local(add_kernel, "add", sum_next, came_next)
    other_own = exchange(sum_next, 1)
    sum_own = local(add_kernel, "add", sum_own, came_own)
    other_next = exchange(sum_own, 1)
    key_own = local(square_kernel, "square", sum_own, other_own)
    key_first = exchange(key_own, 0)
    key_next = local(square_kernel, "square", sum_next, other_next)
    keys = key_own, key_next, key_first, exchange(key_next, 0)

    def out_part(half, which, bank, kept, *done):
        out = sum(d.shape[0] for d in done) + len(which), 2, tok, feat
        return call(
            functools.partial(out_kernel, half, which), "out_part", [(out, kept)],
            [SMEM] * 2 + [VMEM] * (len(which) + 3 + len(done)), cost(len(which) * quarter, wide, feat),
            (order, ids, *[keys[i] for i in which], value_all, bank, hidden, *done),
        )[0]

    rest = out_part(1, (0, 1, 2), bank_other, jnp.bfloat16)
    came = swap(out_part(1, (3,), bank_other, jnp.bfloat16, rest))
    result = call(
        place_kernel, "place", [((NY, tok, feat), jnp.bfloat16)], [SMEM] * 2 + [VMEM] * 2,
        cost(NY * tok, 1, feat), (order, at, out_part(0, (0, 1, 2, 3), dim_bank, jnp.float32), came),
    )[0]
    result, everyone = lax.optimization_barrier((result, everyone))
    pieces = lax.all_to_all(result, YQ + ("y_low",), 0, 0)
    outputs = jnp.sum(pieces.astype(jnp.float32), axis=0).astype(jnp.bfloat16)
    key_step, value_step = call(
        step_kernel, "steps", [(key_weight.shape, jnp.float32), (value_weight.shape, jnp.float32)],
        [SMEM] + [VMEM] * 3, cost(hid, 512, feat), (at, everyone, dim_bank, hidden_bank),
    )
    return outputs, key_step, value_step


def solution(mesh):
    axes = ("z", "y_hi", "y_mid", "y_low", "x", "core")
    fine = Mesh(mesh.devices.reshape(8, 2, 2, 2, 4, 2), axes)
    pop, row, col = ("z", "y_hi"), ("y_mid", "y_low"), ("x", "core")
    in_specs = (
        P(pop + row, col),
        P(col),
        P(col, row + pop),
        P(row + pop, col),
        P(None, col),
        P(None, row),
        P(pop + row, None),
        P(pop + row),
    )
    out_specs = (P(pop + row, col), P(col, row + pop), P(row + pop, col))
    return jax.shard_map(shards, mesh=fine, in_specs=in_specs, out_specs=out_specs, check_vma=False)
```

```python
import functools

import jax
import jax.numpy as jnp
from jax import lax
from jax.experimental import pallas as pl
from jax.experimental.pallas import tpu as pltpu
from jax.sharding import Mesh
from jax.sharding import PartitionSpec as P

D = 4096
FF = 16384
BATCH = 64
MEMBERS = 128
NY, NQ = 8, 4
NX, NZ = 4, 8
INFO = 16
YQ = ("y_hi", "y_mid")
HIGH = lax.Precision.HIGHEST
SIGMA_K = 0.5 / D**0.5
SIGMA_V = 0.5 / FF**0.5
VMEM = pl.BlockSpec(memory_space=pltpu.VMEM)
HBM = pl.BlockSpec(memory_space=pltpu.HBM)
ANY = pl.BlockSpec(memory_space=pl.ANY)
SMEM = pl.BlockSpec(memory_space=pltpu.SMEM)


def swap(x):
    return lax.ppermute(x, "core", [(0, 1), (1, 0)])


def exchange(x, second):
    pairs = []
    for i in range(NX):
        for core in range(2):
            to = i ^ 1 if core == second else NX - 1 - i
            pairs.append((2 * i + core, 2 * to + core))
    return lax.ppermute(x, ("x", "core"), pairs)


def beside(x):
    pairs = []
    for y in range(NY):
        for core in range(2):
            to = y ^ 1 if core == 0 else (y + 2 * (y % 2) - 1) % NY
            pairs.append((2 * y + core, 2 * to + core))
    return lax.ppermute(x, YQ + ("y_low", "core"), pairs)


def shift_kernel(copies, picks_hbm, ranks_hbm, x_hbm, mix_hbm, out_ref, picks_ref, ranks_ref, x_ref, mix_ref, sems):
    pairs = (x_hbm, x_ref), (mix_hbm, mix_ref), (picks_hbm, picks_ref), (ranks_hbm, ranks_ref)
    fetches = [pltpu.make_async_copy(src, dst, sems.at[i]) for i, (src, dst) in enumerate(pairs)]
    for fetch in fetches:
        fetch.start()
    for fetch in fetches:
        fetch.wait()
    tok, feat = x_ref.shape
    values = x_ref[...].astype(jnp.float32)
    first = lax.broadcasted_iota(jnp.int32, values.shape, 0) % BATCH == 0
    previous = jnp.where(first, 0.0, pltpu.roll(values, 1, 0))
    shifted = (values + (previous - values) * mix_ref[...]).astype(jnp.bfloat16)
    row = lax.broadcasted_iota(jnp.int32, (INFO, feat), 0)
    lane = lax.broadcasted_iota(jnp.int32, (INFO, feat), 1)
    info = jnp.zeros((INFO, feat), jnp.float32)
    for i in range(tok // BATCH):
        entries = [picks_ref[i, j] for j in range(4)] + [ranks_ref[i]]
        for j, entry in enumerate(entries):
            info = jnp.where((row == i) & (lane == j), entry.astype(jnp.float32), info)
    info = info.astype(jnp.bfloat16)
    for i in range(copies):
        out_ref[i, :tok, :] = shifted
        out_ref[i, tok:, :] = info


def hidden_kernel(at_ref, hid_hbm, out_ref, sems):
    apart, width = hid_hbm.shape[1] // NZ, out_ref.shape[1] // NZ
    fetches = []
    for i in range(NZ):
        start = pl.multiple_of(at_ref[0] + i * apart, width)
        src, dst = hid_hbm.at[:, pl.ds(start, width)], out_ref.at[:, pl.ds(i * width, width)]
        fetches.append(pltpu.make_async_copy(src, dst, sems.at[i]))
        fetches[-1].start()
    for fetch in fetches:
        fetch.wait()


def key_kernel(order, order_ref, ids_ref, *refs):
    tokens, (w_ref, bank_ref, other_ref, hid_ref, *out_refs) = refs[:4], refs[4:]
    tok = tokens[0].shape[1] - INFO
    own = tok // BATCH
    blocks, inner, picks = [], [], []
    for i in order:
        u = order_ref[i]
        for s in range(2):
            for j in range(own):
                rows = [r[u, j * BATCH : (j + 1) * BATCH, :] for r in (tokens[s], tokens[2 + s])]
                m = (s * NX + u) * own + j
                fac_a = [r[pl.ds(ids_ref[m, 0], 1), :] for r in (bank_ref, other_ref)]
                dots = sum(r.astype(jnp.float32) * a for r, a in zip(rows, fac_a))
                inner.append(SIGMA_K * jnp.sum(dots, axis=1, keepdims=True))
                picks.append(ids_ref[m, 1])
                blocks.append(jnp.concatenate(rows, axis=1))
    rows = jnp.concatenate(blocks, axis=0)
    width, per = w_ref.shape[2], 2 * own
    for n in range(0, NZ, 2):
        cols = slice(n * width, (n + 2) * width)
        w = jnp.concatenate([w_ref[n], w_ref[n + 1]], axis=1)
        acc = jnp.dot(rows, w, preferred_element_type=jnp.float32)
        for k, (part, pick) in enumerate(zip(inner, picks)):
            term = acc[k * BATCH : (k + 1) * BATCH] + part * hid_ref[pl.ds(pick, 1), cols]
            i, at = divmod(k, per)
            out_refs[i][at * BATCH : (at + 1) * BATCH, cols] = term.astype(out_refs[i].dtype)


def add_kernel(kept_ref, came_ref, out_ref):
    out_ref[...] = (kept_ref[...] + came_ref[...].astype(jnp.float32)).astype(jnp.bfloat16)


def square_kernel(mine_ref, came_ref, out_ref):
    total = mine_ref[...].astype(jnp.float32) + came_ref[...].astype(jnp.float32)
    out_ref[...] = (jnp.maximum(total, 0.0) ** 2).astype(jnp.bfloat16)


def out_kernel(half, order, order_ref, ids_ref, *refs):
    keys, (v_ref, bank_ref, hid_ref, *_, out_ref) = refs[: len(order)], refs[len(order) :]
    feat, width = out_ref.shape[3], hid_ref.shape[1] // NZ
    tok = out_ref.shape[2]
    own, wide = tok // BATCH, 256
    inner, picks, places = [], [], []
    for i, o in enumerate(order):
        for s in range(2):
            for j in range(own):
                m = (s * NX + order_ref[o]) * own + j
                fac_c = hid_ref[pl.ds(ids_ref[m, 2], 1), :]
                at = s * tok + j * BATCH
                part = keys[i][at : at + BATCH, :].astype(jnp.float32)
                inner.append(SIGMA_V * jnp.sum(part * fac_c, axis=1, keepdims=True))
                picks.append(ids_ref[m, 3])
                places.append((i, s, slice(j * BATCH, (j + 1) * BATCH)))
    rows = jnp.concatenate([k[...] for k in keys], axis=0)
    for n in range(feat // wide):
        cols = slice(n * wide, (n + 1) * wide)
        from_v = slice(half * feat + n * wide, half * feat + (n + 1) * wide)
        v = jnp.concatenate([v_ref[i, :width, from_v] for i in range(NZ)], axis=0)
        acc = jnp.dot(rows, v, preferred_element_type=jnp.float32)
        for k, (i, s, at) in enumerate(places):
            part = acc[k * BATCH : (k + 1) * BATCH] + inner[k] * bank_ref[pl.ds(picks[k], 1), cols]
            out_ref[i, s, at, cols] = part.astype(out_ref.dtype)


def place_kernel(orders, order_ref, at_ref, *refs):
    parts, out_ref = refs[:-1], refs[-1]
    twins = (0, 2, 1)
    for order, mine_ref, came_ref in zip(orders, parts[::2], parts[1::2]):
        for i, o in enumerate(order):
            for s in range(2):
                total = mine_ref[i, s] + came_ref[twins[i], s].astype(jnp.float32)
                out_ref[2 * order_ref[o] + lax.rem(at_ref[2] + s, 2)] = total.astype(jnp.bfloat16)


def step_kernel(at_ref, info_ref, bank_ref, hid_ref, key_ref, value_ref):
    info = info_ref[...].astype(jnp.float32)
    fitness = 2.0 * info[:, 4:5] / (MEMBERS - 1) - 1.0
    fitness = fitness * (1.0 / MEMBERS**0.5)
    lane = lax.broadcasted_iota(jnp.int32, (info.shape[0], bank_ref.shape[0]), 1).astype(jnp.float32)
    pick = [(info[:, i : i + 1] == lane).astype(jnp.float32) for i in range(4)]
    hid = key_ref.shape[1]
    hidden = hid_ref[:, pl.ds(pl.multiple_of(at_ref[1], hid), hid)]

    def product(a, b, contract):
        dims = ((contract,), (0,)), ((), ())
        return lax.dot_general(a, b, dims, precision=HIGH, preferred_element_type=jnp.float32)

    pair_k = product(fitness * pick[0], pick[1], 0)
    pair_v = product(fitness * pick[2], pick[3], 0)
    key_ref[...] = product(bank_ref[...], product(pair_k, hidden, 1), 0)
    value_ref[...] = product(hidden, product(pair_v, bank_ref[...], 1), 0)


def cost(rows, depth, cols):
    return pl.CostEstimate(
        flops=2 * rows * depth * cols,
        bytes_accessed=2 * (rows * depth + depth * cols + rows * cols),
        transcendentals=0,
    )


def call(kernel, name, outs, specs, estimate, args, scratch=()):
    args = [pltpu.with_memory_space_constraint(a, pltpu.HBM) if s is HBM else a for a, s in zip(args, specs)]
    return pl.pallas_call(
        kernel,
        out_shape=[jax.ShapeDtypeStruct(*out) for out in outs],
        in_specs=specs,
        out_specs=[VMEM] * len(outs),
        scratch_shapes=scratch,
        compiler_params=pltpu.CompilerParams(vmem_limit_bytes=16 << 20),
        cost_estimate=estimate,
        name=name,
    )(*args)


def shards(inputs, mix, key_weight, value_weight, dim_bank, hidden_bank, member_picks, ranks):
    tok, feat = inputs.shape
    hid = key_weight.shape[1]
    half = hid // 2
    own = tok // BATCH
    core, x, z = lax.axis_index("core"), lax.axis_index("x"), lax.axis_index("z")
    block = (z * 2 + lax.axis_index("y_hi")) * hid
    at = [lax.axis_index("y_hi") * hid + core * half, block, lax.axis_index("y_low")]
    at = jnp.stack(at).astype(jnp.int32)

    key_other, value_other, bank_other = swap(key_weight), swap(value_weight), swap(dim_bank)
    scratch = [
        pltpu.SMEM(member_picks.shape, jnp.int32), pltpu.SMEM(ranks.shape, jnp.int32),
        pltpu.VMEM(inputs.shape, jnp.bfloat16), pltpu.VMEM((1, feat), jnp.float32),
        pltpu.SemaphoreType.DMA((4,)),
    ]
    shifted = call(
        functools.partial(shift_kernel, NQ), "shift", [((NQ, tok + INFO, feat), jnp.bfloat16)],
        [HBM] * 4, cost(tok, 16, feat), (member_picks, ranks, inputs, mix[None]), scratch,
    )[0]
    same = lax.all_to_all(shifted, YQ, 0, 0)
    other = beside(same)
    tokens = same, other, swap(same), swap(other)
    members = NY * own
    info = jnp.stack([t[:, tok : tok + own, :128] for t in (same, other)]).reshape(members, 128)
    ids = info[:, :4].astype(jnp.int32)

    def hidden_half(array, axis):
        return lax.dynamic_slice_in_dim(array, core * half, half, axis)

    key_pack = jnp.concatenate([hidden_half(key_weight, 1), hidden_half(key_other, 1)], axis=0)
    key_all = lax.all_gather(key_pack, "z", axis=0)
    value_other, bank_other = lax.optimization_barrier((value_other, bank_other))
    value_pack = jnp.concatenate([hidden_half(value_weight, 0), hidden_half(value_other, 0)], axis=1)
    info = jnp.pad(info, ((0, INFO - members), (0, 2 * feat - 128)))
    value_all = lax.all_gather(jnp.concatenate([value_pack, info], axis=0), "z", axis=0)
    everyone = value_all[:, half : half + members, :128].reshape(NZ * members, 128)

    before, after = NX - 1 - x, x + 1 - 2 * lax.rem(x, 2)
    order = [x, jnp.where(core == 0, before, after), jnp.where(core == 0, after, before), lax.rem(x + 2, NX)]
    order = jnp.stack(order).astype(jnp.int32)
    deep, wide, quarter = 2 * feat, NZ * half, NY * tok // NX
    low, high = ((quarter, wide), jnp.bfloat16), ((quarter, wide), jnp.float32)
    hidden = call(
        hidden_kernel, "hidden", [((hidden_bank.shape[0], wide), jnp.float32)], [SMEM, HBM],
        cost(hidden_bank.shape[0], 1, wide), (at, hidden_bank), [pltpu.SemaphoreType.DMA((NZ,))],
    )[0]

    def key_part(which, outs):
        return call(
            functools.partial(key_kernel, which), "key_part", outs,
            [SMEM] * 2 + [VMEM] * 8, cost(len(which) * quarter, deep, wide),
            (order, ids, *tokens, key_all, dim_bank, bank_other, hidden),
        )

    def local(kernel, name, *args):
        return call(kernel, name, [low], [VMEM] * len(args), cost(quarter, 4, wide), args)[0]

    came_next = exchange(key_part((3,), [low])[0], 0)
    came_own = exchange(key_part((2,), [low])[0], 0)
    sum_next, sum_own = key_part((1, 0), [high, high])
    sum_next = local(add_kernel, "add", sum_next, came_next)
    other_own = exchange(sum_next, 1)
    sum_own = local(add_kernel, "add", sum_own, came_own)
    other_next = exchange(sum_own, 1)
    key_own = local(square_kernel, "square", sum_own, other_own)
    key_first = exchange(key_own, 0)
    key_next = local(square_kernel, "square", sum_next, other_next)
    keys = key_own, key_next, key_first, exchange(key_next, 0)

    def out_part(half, which, bank, kept, *after):
        out = len(which), 2, tok, feat
        return call(
            functools.partial(out_kernel, half, which), "out_part", [(out, kept)],
            [SMEM] * 2 + [VMEM] * (len(which) + 3) + [ANY] * len(after), cost(len(which) * quarter, wide, feat),
            (order, ids, *[keys[i] for i in which], value_all, bank, hidden, *after),
        )[0]

    sets = (0, 1, 2), (3,)
    parts = []
    for which in sets:
        came = swap(out_part(1, which, bank_other, jnp.bfloat16, *parts[:1]))
        parts += [out_part(0, which, dim_bank, jnp.float32), came]
    result = call(
        functools.partial(place_kernel, sets), "place", [((NY, tok, feat), jnp.bfloat16)],
        [SMEM] * 2 + [VMEM] * 4, cost(NY * tok, 1, feat), (order, at, *parts),
    )[0]
    result, everyone = lax.optimization_barrier((result, everyone))
    pieces = lax.all_to_all(result, YQ + ("y_low",), 0, 0)
    outputs = jnp.sum(pieces.astype(jnp.float32), axis=0).astype(jnp.bfloat16)
    key_step, value_step = call(
        step_kernel, "steps", [(key_weight.shape, jnp.float32), (value_weight.shape, jnp.float32)],
        [SMEM] + [VMEM] * 3, cost(hid, 512, feat), (at, everyone, dim_bank, hidden_bank),
    )
    return outputs, key_step, value_step


def solution(mesh):
    axes = ("z", "y_hi", "y_mid", "y_low", "x", "core")
    fine = Mesh(mesh.devices.reshape(8, 2, 2, 2, 4, 2), axes)
    pop, row, col = ("z", "y_hi"), ("y_mid", "y_low"), ("x", "core")
    in_specs = (
        P(pop + row, col),
        P(col),
        P(col, row + pop),
        P(row + pop, col),
        P(None, col),
        P(None, row),
        P(pop + row, None),
        P(pop + row),
    )
    out_specs = (P(pop + row, col), P(col, row + pop), P(row + pop, col))
    return jax.shard_map(shards, mesh=fine, in_specs=in_specs, out_specs=out_specs, check_vma=False)
```

```python
import functools

import jax
import jax.numpy as jnp
from jax import lax
from jax.experimental import pallas as pl
from jax.experimental.pallas import tpu as pltpu
from jax.sharding import Mesh
from jax.sharding import PartitionSpec as P

D = 4096
FF = 16384
BATCH = 64
MEMBERS = 128
NY, NQ = 8, 4
NX, NZ = 4, 8
INFO = 16
YQ = ("y_hi", "y_mid")
HIGH = lax.Precision.HIGHEST
SIGMA_K = 0.5 / D**0.5
SIGMA_V = 0.5 / FF**0.5
VMEM = pl.BlockSpec(memory_space=pltpu.VMEM)
HBM = pl.BlockSpec(memory_space=pltpu.HBM)
ANY = pl.BlockSpec(memory_space=pl.ANY)
SMEM = pl.BlockSpec(memory_space=pltpu.SMEM)


def swap(x):
    return lax.ppermute(x, "core", [(0, 1), (1, 0)])


def exchange(x, second):
    pairs = []
    for i in range(NX):
        for core in range(2):
            to = i ^ 1 if core == second else NX - 1 - i
            pairs.append((2 * i + core, 2 * to + core))
    return lax.ppermute(x, ("x", "core"), pairs)


def beside(x):
    pairs = []
    for y in range(NY):
        for core in range(2):
            to = y ^ 1 if core == 0 else (y + 2 * (y % 2) - 1) % NY
            pairs.append((2 * y + core, 2 * to + core))
    return lax.ppermute(x, YQ + ("y_low", "core"), pairs)


def shift_kernel(copies, picks_hbm, ranks_hbm, x_hbm, mix_hbm, out_ref, picks_ref, ranks_ref, x_ref, mix_ref, sems):
    pairs = (x_hbm, x_ref), (mix_hbm, mix_ref), (picks_hbm, picks_ref), (ranks_hbm, ranks_ref)
    fetches = [pltpu.make_async_copy(src, dst, sems.at[i]) for i, (src, dst) in enumerate(pairs)]
    for fetch in fetches:
        fetch.start()
    for fetch in fetches:
        fetch.wait()
    tok, feat = x_ref.shape
    values = x_ref[...].astype(jnp.float32)
    first = lax.broadcasted_iota(jnp.int32, values.shape, 0) % BATCH == 0
    previous = jnp.where(first, 0.0, pltpu.roll(values, 1, 0))
    shifted = (values + (previous - values) * mix_ref[...]).astype(jnp.bfloat16)
    row = lax.broadcasted_iota(jnp.int32, (INFO, feat), 0)
    lane = lax.broadcasted_iota(jnp.int32, (INFO, feat), 1)
    info = jnp.zeros((INFO, feat), jnp.float32)
    for i in range(tok // BATCH):
        entries = [picks_ref[i, j] for j in range(4)] + [ranks_ref[i]]
        for j, entry in enumerate(entries):
            info = jnp.where((row == i) & (lane == j), entry.astype(jnp.float32), info)
    info = info.astype(jnp.bfloat16)
    for i in range(copies):
        out_ref[i, :tok, :] = shifted
        out_ref[i, tok:, :] = info


def copy_kernel(x_ref, _, out_ref):
    out_ref[...] = x_ref[...]


def hidden_kernel(at_ref, hid_hbm, out_ref, sems):
    apart, width = hid_hbm.shape[1] // NZ, out_ref.shape[1] // NZ
    fetches = []
    for i in range(NZ):
        start = pl.multiple_of(at_ref[0] + i * apart, width)
        src, dst = hid_hbm.at[:, pl.ds(start, width)], out_ref.at[:, pl.ds(i * width, width)]
        fetches.append(pltpu.make_async_copy(src, dst, sems.at[i]))
        fetches[-1].start()
    for fetch in fetches:
        fetch.wait()


def key_kernel(order, order_ref, ids_ref, *refs):
    tokens, (w_ref, bank_ref, other_ref, hid_ref, *out_refs) = refs[:4], refs[4:]
    tok = tokens[0].shape[1] - INFO
    own = tok // BATCH
    blocks, inner, picks = [], [], []
    for i in order:
        u = order_ref[i]
        for s in range(2):
            for j in range(own):
                rows = [r[u, j * BATCH : (j + 1) * BATCH, :] for r in (tokens[s], tokens[2 + s])]
                m = (s * NX + u) * own + j
                fac_a = [r[pl.ds(ids_ref[m, 0], 1), :] for r in (bank_ref, other_ref)]
                dots = sum(r.astype(jnp.float32) * a for r, a in zip(rows, fac_a))
                inner.append(SIGMA_K * jnp.sum(dots, axis=1, keepdims=True))
                picks.append(ids_ref[m, 1])
                blocks.append(jnp.concatenate(rows, axis=1))
    rows = jnp.concatenate(blocks, axis=0)
    width, per = w_ref.shape[2], 2 * own
    for n in range(0, NZ, 2):
        cols = slice(n * width, (n + 2) * width)
        w = jnp.concatenate([w_ref[n], w_ref[n + 1]], axis=1)
        acc = jnp.dot(rows, w, preferred_element_type=jnp.float32)
        for k, (part, pick) in enumerate(zip(inner, picks)):
            term = acc[k * BATCH : (k + 1) * BATCH] + part * hid_ref[pl.ds(pick, 1), cols]
            i, at = divmod(k, per)
            out_refs[i][at * BATCH : (at + 1) * BATCH, cols] = term.astype(out_refs[i].dtype)


def add_kernel(kept_ref, came_ref, out_ref):
    out_ref[...] = (kept_ref[...] + came_ref[...].astype(jnp.float32)).astype(jnp.bfloat16)


def square_kernel(mine_ref, came_ref, out_ref):
    total = mine_ref[...].astype(jnp.float32) + came_ref[...].astype(jnp.float32)
    out_ref[...] = (jnp.maximum(total, 0.0) ** 2).astype(jnp.bfloat16)


def out_kernel(half, order, order_ref, ids_ref, *refs):
    keys, (v_ref, bank_ref, hid_ref, *done, out_ref) = refs[: len(order)], refs[len(order) :]
    feat, width = out_ref.shape[3], hid_ref.shape[1] // NZ
    tok = out_ref.shape[2]
    own, wide = tok // BATCH, 256
    for ref in done:
        out_ref[: ref.shape[0]] = ref[...]
    inner, picks, places = [], [], []
    for i, o in enumerate(order):
        for s in range(2):
            for j in range(own):
                m = (s * NX + order_ref[o]) * own + j
                fac_c = hid_ref[pl.ds(ids_ref[m, 2], 1), :]
                at = s * tok + j * BATCH
                part = keys[i][at : at + BATCH, :].astype(jnp.float32)
                inner.append(SIGMA_V * jnp.sum(part * fac_c, axis=1, keepdims=True))
                picks.append(ids_ref[m, 3])
                places.append((out_ref.shape[0] - len(order) + i, s, slice(j * BATCH, (j + 1) * BATCH)))
    rows = jnp.concatenate([k[...] for k in keys], axis=0)
    for n in range(feat // wide):
        cols = slice(n * wide, (n + 1) * wide)
        from_v = slice(half * feat + n * wide, half * feat + (n + 1) * wide)
        v = jnp.concatenate([v_ref[i, :width, from_v] for i in range(NZ)], axis=0)
        acc = jnp.dot(rows, v, preferred_element_type=jnp.float32)
        for k, (i, s, at) in enumerate(places):
            part = acc[k * BATCH : (k + 1) * BATCH] + inner[k] * bank_ref[pl.ds(picks[k], 1), cols]
            out_ref[i, s, at, cols] = part.astype(out_ref.dtype)


def place_kernel(order_ref, at_ref, mine_ref, came_ref, out_ref):
    twins = (0, 2, 1, 3)
    for i in range(NX):
        for s in range(2):
            total = mine_ref[i, s] + came_ref[twins[i], s].astype(jnp.float32)
            out_ref[2 * order_ref[i] + lax.rem(at_ref[2] + s, 2)] = total.astype(jnp.bfloat16)


def step_kernel(at_ref, info_ref, bank_ref, hid_ref, key_ref, value_ref):
    info = info_ref[...].astype(jnp.float32)
    fitness = 2.0 * info[:, 4:5] / (MEMBERS - 1) - 1.0
    fitness = fitness * (1.0 / MEMBERS**0.5)
    lane = lax.broadcasted_iota(jnp.int32, (info.shape[0], bank_ref.shape[0]), 1).astype(jnp.float32)
    pick = [(info[:, i : i + 1] == lane).astype(jnp.float32) for i in range(4)]
    hid = key_ref.shape[1]
    hidden = hid_ref[:, pl.ds(pl.multiple_of(at_ref[1], hid), hid)]

    def product(a, b, contract):
        dims = ((contract,), (0,)), ((), ())
        return lax.dot_general(a, b, dims, precision=HIGH, preferred_element_type=jnp.float32)

    pair_k = product(fitness * pick[0], pick[1], 0)
    pair_v = product(fitness * pick[2], pick[3], 0)
    key_ref[...] = product(bank_ref[...], product(pair_k, hidden, 1), 0)
    value_ref[...] = product(hidden, product(pair_v, bank_ref[...], 1), 0)


def cost(rows, depth, cols):
    return pl.CostEstimate(
        flops=2 * rows * depth * cols,
        bytes_accessed=2 * (rows * depth + depth * cols + rows * cols),
        transcendentals=0,
    )


def call(kernel, name, outs, specs, estimate, args, scratch=()):
    args = [pltpu.with_memory_space_constraint(a, pltpu.HBM) if s is HBM else a for a, s in zip(args, specs)]
    return pl.pallas_call(
        kernel,
        out_shape=[jax.ShapeDtypeStruct(*out) for out in outs],
        in_specs=specs,
        out_specs=[VMEM] * len(outs),
        scratch_shapes=scratch,
        compiler_params=pltpu.CompilerParams(vmem_limit_bytes=16 << 20),
        cost_estimate=estimate,
        name=name,
    )(*args)


def shards(inputs, mix, key_weight, value_weight, dim_bank, hidden_bank, member_picks, ranks):
    tok, feat = inputs.shape
    hid = key_weight.shape[1]
    half = hid // 2
    own = tok // BATCH
    core, x, z = lax.axis_index("core"), lax.axis_index("x"), lax.axis_index("z")
    block = (z * 2 + lax.axis_index("y_hi")) * hid
    at = [lax.axis_index("y_hi") * hid + core * half, block, lax.axis_index("y_low")]
    at = jnp.stack(at).astype(jnp.int32)

    key_other, value_other = swap(key_weight), swap(value_weight)
    scratch = [
        pltpu.SMEM(member_picks.shape, jnp.int32), pltpu.SMEM(ranks.shape, jnp.int32),
        pltpu.VMEM(inputs.shape, jnp.bfloat16), pltpu.VMEM((1, feat), jnp.float32),
        pltpu.SemaphoreType.DMA((4,)),
    ]
    shifted = call(
        functools.partial(shift_kernel, NQ), "shift", [((NQ, tok + INFO, feat), jnp.bfloat16)],
        [HBM] * 4, cost(tok, 16, feat), (member_picks, ranks, inputs, mix[None]), scratch,
    )[0]
    same = lax.all_to_all(shifted, YQ, 0, 0)
    other = beside(same)
    tokens = same, other, swap(same), swap(other)
    members = NY * own
    info = jnp.stack([t[:, tok : tok + own, :128] for t in (same, other)]).reshape(members, 128)
    ids = info[:, :4].astype(jnp.int32)

    def hidden_half(array, axis):
        return lax.dynamic_slice_in_dim(array, core * half, half, axis)

    key_pack = jnp.concatenate([hidden_half(key_weight, 1), hidden_half(key_other, 1)], axis=0)
    key_all = lax.all_gather(key_pack, "z", axis=0)
    bank_other = swap(call(
        copy_kernel, "bank", [(dim_bank.shape, jnp.float32)], [VMEM, ANY], cost(dim_bank.shape[0], 1, feat),
        (dim_bank, key_all),
    )[0])
    value_pack = jnp.concatenate([hidden_half(value_weight, 0), hidden_half(value_other, 0)], axis=1)
    info = jnp.pad(info, ((0, INFO - members), (0, 2 * feat - 128)))
    value_all = lax.all_gather(jnp.concatenate([value_pack, info], axis=0), "z", axis=0)
    everyone = value_all[:, half : half + members, :128].reshape(NZ * members, 128)

    before, after = NX - 1 - x, x + 1 - 2 * lax.rem(x, 2)
    order = [x, jnp.where(core == 0, before, after), jnp.where(core == 0, after, before), lax.rem(x + 2, NX)]
    order = jnp.stack(order).astype(jnp.int32)
    deep, wide, quarter = 2 * feat, NZ * half, NY * tok // NX
    low, high = ((quarter, wide), jnp.bfloat16), ((quarter, wide), jnp.float32)
    hidden = call(
        hidden_kernel, "hidden", [((hidden_bank.shape[0], wide), jnp.float32)], [SMEM, HBM],
        cost(hidden_bank.shape[0], 1, wide), (at, hidden_bank), [pltpu.SemaphoreType.DMA((NZ,))],
    )[0]

    def key_part(which, outs):
        return call(
            functools.partial(key_kernel, which), "key_part", outs,
            [SMEM] * 2 + [VMEM] * 8, cost(len(which) * quarter, deep, wide),
            (order, ids, *tokens, key_all, dim_bank, bank_other, hidden),
        )

    def local(kernel, name, *args):
        return call(kernel, name, [low], [VMEM] * len(args), cost(quarter, 4, wide), args)[0]

    came_next = exchange(key_part((3,), [low])[0], 0)
    came_own = exchange(key_part((2,), [low])[0], 0)
    sum_next, sum_own = key_part((1, 0), [high, high])
    sum_next = local(add_kernel, "add", sum_next, came_next)
    other_own = exchange(sum_next, 1)
    sum_own = local(add_kernel, "add", sum_own, came_own)
    other_next = exchange(sum_own, 1)
    key_own = local(square_kernel, "square", sum_own, other_own)
    key_first = exchange(key_own, 0)
    key_next = local(square_kernel, "square", sum_next, other_next)
    keys = key_own, key_next, key_first, exchange(key_next, 0)

    def out_part(half, which, bank, kept, *done):
        out = sum(d.shape[0] for d in done) + len(which), 2, tok, feat
        return call(
            functools.partial(out_kernel, half, which), "out_part", [(out, kept)],
            [SMEM] * 2 + [VMEM] * (len(which) + 3 + len(done)), cost(len(which) * quarter, wide, feat),
            (order, ids, *[keys[i] for i in which], value_all, bank, hidden, *done),
        )[0]

    rest = out_part(1, (0, 1, 2), bank_other, jnp.bfloat16)
    came = swap(out_part(1, (3,), bank_other, jnp.bfloat16, rest))
    result = call(
        place_kernel, "place", [((NY, tok, feat), jnp.bfloat16)], [SMEM] * 2 + [VMEM] * 2,
        cost(NY * tok, 1, feat), (order, at, out_part(0, (0, 1, 2, 3), dim_bank, jnp.float32), came),
    )[0]
    result, everyone = lax.optimization_barrier((result, everyone))
    pieces = lax.all_to_all(result, YQ + ("y_low",), 0, 0)
    outputs = jnp.sum(pieces.astype(jnp.float32), axis=0).astype(jnp.bfloat16)
    key_step, value_step = call(
        step_kernel, "steps", [(key_weight.shape, jnp.float32), (value_weight.shape, jnp.float32)],
        [SMEM] + [VMEM] * 3, cost(hid, 512, feat), (at, everyone, dim_bank, hidden_bank),
    )
    return outputs, key_step, value_step


def solution(mesh):
    axes = ("z", "y_hi", "y_mid", "y_low", "x", "core")
    fine = Mesh(mesh.devices.reshape(8, 2, 2, 2, 4, 2), axes)
    pop, row, col = ("z", "y_hi"), ("y_mid", "y_low"), ("x", "core")
    in_specs = (
        P(pop + row, col),
        P(col),
        P(col, row + pop),
        P(row + pop, col),
        P(None, col),
        P(None, row),
        P(pop + row, None),
        P(pop + row),
    )
    out_specs = (P(pop + row, col), P(col, row + pop), P(row + pop, col))
    return jax.shard_map(shards, mesh=fine, in_specs=in_specs, out_specs=out_specs, check_vma=False)
```

```python
import functools

import jax
import jax.numpy as jnp
from jax import lax
from jax.experimental import pallas as pl
from jax.experimental.pallas import tpu as pltpu
from jax.sharding import Mesh
from jax.sharding import PartitionSpec as P

D = 4096
FF = 16384
BATCH = 64
MEMBERS = 128
NY, NQ = 8, 4
NX, NZ = 4, 8
INFO = 16
YQ = ("y_hi", "y_mid")
HIGH = lax.Precision.HIGHEST
SIGMA_K = 0.5 / D**0.5
SIGMA_V = 0.5 / FF**0.5
VMEM = pl.BlockSpec(memory_space=pltpu.VMEM)
HBM = pl.BlockSpec(memory_space=pltpu.HBM)
ANY = pl.BlockSpec(memory_space=pl.ANY)
SMEM = pl.BlockSpec(memory_space=pltpu.SMEM)


def swap(x):
    return lax.ppermute(x, "core", [(0, 1), (1, 0)])


def exchange(x, second):
    pairs = []
    for i in range(NX):
        for core in range(2):
            to = i ^ 1 if core == second else NX - 1 - i
            pairs.append((2 * i + core, 2 * to + core))
    return lax.ppermute(x, ("x", "core"), pairs)


def beside(x):
    pairs = []
    for y in range(NY):
        for core in range(2):
            to = y ^ 1 if core == 0 else (y + 2 * (y % 2) - 1) % NY
            pairs.append((2 * y + core, 2 * to + core))
    return lax.ppermute(x, YQ + ("y_low", "core"), pairs)


def shift_kernel(copies, picks_hbm, ranks_hbm, x_hbm, mix_hbm, out_ref, picks_ref, ranks_ref, x_ref, mix_ref, sems):
    pairs = (x_hbm, x_ref), (mix_hbm, mix_ref), (picks_hbm, picks_ref), (ranks_hbm, ranks_ref)
    fetches = [pltpu.make_async_copy(src, dst, sems.at[i]) for i, (src, dst) in enumerate(pairs)]
    for fetch in fetches:
        fetch.start()
    for fetch in fetches:
        fetch.wait()
    tok, feat = x_ref.shape
    values = x_ref[...].astype(jnp.float32)
    first = lax.broadcasted_iota(jnp.int32, values.shape, 0) % BATCH == 0
    previous = jnp.where(first, 0.0, pltpu.roll(values, 1, 0))
    shifted = (values + (previous - values) * mix_ref[...]).astype(jnp.bfloat16)
    row = lax.broadcasted_iota(jnp.int32, (INFO, feat), 0)
    lane = lax.broadcasted_iota(jnp.int32, (INFO, feat), 1)
    info = jnp.zeros((INFO, feat), jnp.float32)
    for i in range(tok // BATCH):
        entries = [picks_ref[i, j] for j in range(4)] + [ranks_ref[i]]
        for j, entry in enumerate(entries):
            info = jnp.where((row == i) & (lane == j), entry.astype(jnp.float32), info)
    info = info.astype(jnp.bfloat16)
    for i in range(copies):
        out_ref[i, :tok, :] = shifted
        out_ref[i, tok:, :] = info


def copy_kernel(x_ref, _, out_ref):
    out_ref[...] = x_ref[...]


def hidden_kernel(at_ref, hid_hbm, out_ref, sems):
    apart, width = hid_hbm.shape[1] // NZ, out_ref.shape[1] // NZ
    fetches = []
    for i in range(NZ):
        start = pl.multiple_of(at_ref[0] + i * apart, width)
        src, dst = hid_hbm.at[:, pl.ds(start, width)], out_ref.at[:, pl.ds(i * width, width)]
        fetches.append(pltpu.make_async_copy(src, dst, sems.at[i]))
        fetches[-1].start()
    for fetch in fetches:
        fetch.wait()


def key_kernel(order, order_ref, ids_ref, *refs):
    tokens, (w_ref, bank_ref, other_ref, hid_ref, *out_refs) = refs[:4], refs[4:]
    tok = tokens[0].shape[1] - INFO
    own = tok // BATCH
    blocks, inner, picks = [], [], []
    for i in order:
        u = order_ref[i]
        for s in range(2):
            for j in range(own):
                rows = [r[u, j * BATCH : (j + 1) * BATCH, :] for r in (tokens[s], tokens[2 + s])]
                m = (s * NX + u) * own + j
                fac_a = [r[pl.ds(ids_ref[m, 0], 1), :] for r in (bank_ref, other_ref)]
                dots = sum(r.astype(jnp.float32) * a for r, a in zip(rows, fac_a))
                inner.append(SIGMA_K * jnp.sum(dots, axis=1, keepdims=True))
                picks.append(ids_ref[m, 1])
                blocks.append(jnp.concatenate(rows, axis=1))
    rows = jnp.concatenate(blocks, axis=0)
    width, per = w_ref.shape[2], 2 * own
    for n in range(0, NZ, 2):
        cols = slice(n * width, (n + 2) * width)
        w = jnp.concatenate([w_ref[n], w_ref[n + 1]], axis=1)
        acc = jnp.dot(rows, w, preferred_element_type=jnp.float32)
        for k, (part, pick) in enumerate(zip(inner, picks)):
            term = acc[k * BATCH : (k + 1) * BATCH] + part * hid_ref[pl.ds(pick, 1), cols]
            i, at = divmod(k, per)
            out_refs[i][at * BATCH : (at + 1) * BATCH, cols] = term.astype(out_refs[i].dtype)


def add_kernel(kept_ref, came_ref, out_ref):
    out_ref[...] = (kept_ref[...] + came_ref[...].astype(jnp.float32)).astype(jnp.bfloat16)


def square_kernel(mine_ref, came_ref, out_ref):
    total = mine_ref[...].astype(jnp.float32) + came_ref[...].astype(jnp.float32)
    out_ref[...] = (jnp.maximum(total, 0.0) ** 2).astype(jnp.bfloat16)


def out_kernel(half, order, order_ref, ids_ref, *refs):
    keys, (v_ref, bank_ref, hid_ref, *done, out_ref) = refs[: len(order)], refs[len(order) :]
    feat, width = out_ref.shape[3], hid_ref.shape[1] // NZ
    tok = out_ref.shape[2]
    own, wide = tok // BATCH, 256
    for ref in done:
        out_ref[: ref.shape[0]] = ref[...]
    inner, picks, places = [], [], []
    for i, o in enumerate(order):
        for s in range(2):
            for j in range(own):
                m = (s * NX + order_ref[o]) * own + j
                fac_c = hid_ref[pl.ds(ids_ref[m, 2], 1), :]
                at = s * tok + j * BATCH
                part = keys[i][at : at + BATCH, :].astype(jnp.float32)
                inner.append(SIGMA_V * jnp.sum(part * fac_c, axis=1, keepdims=True))
                picks.append(ids_ref[m, 3])
                places.append((out_ref.shape[0] - len(order) + i, s, slice(j * BATCH, (j + 1) * BATCH)))
    rows = jnp.concatenate([k[...] for k in keys], axis=0)
    for n in range(feat // wide):
        cols = slice(n * wide, (n + 1) * wide)
        from_v = slice(half * feat + n * wide, half * feat + (n + 1) * wide)
        v = jnp.concatenate([v_ref[i, :width, from_v] for i in range(NZ)], axis=0)
        acc = jnp.dot(rows, v, preferred_element_type=jnp.float32)
        for k, (i, s, at) in enumerate(places):
            part = acc[k * BATCH : (k + 1) * BATCH] + inner[k] * bank_ref[pl.ds(picks[k], 1), cols]
            out_ref[i, s, at, cols] = part.astype(out_ref.dtype)


def place_kernel(order_ref, at_ref, mine_ref, came_ref, out_ref):
    twins = (0, 2, 1, 3)
    for i in range(NX):
        for s in range(2):
            total = mine_ref[i, s] + came_ref[twins[i], s].astype(jnp.float32)
            out_ref[2 * order_ref[i] + lax.rem(at_ref[2] + s, 2)] = total.astype(jnp.bfloat16)


def step_kernel(at_ref, info_ref, bank_ref, hid_ref, key_ref, value_ref):
    info = info_ref[...].astype(jnp.float32)
    fitness = 2.0 * info[:, 4:5] / (MEMBERS - 1) - 1.0
    fitness = fitness * (1.0 / MEMBERS**0.5)
    lane = lax.broadcasted_iota(jnp.int32, (info.shape[0], bank_ref.shape[0]), 1).astype(jnp.float32)
    pick = [(info[:, i : i + 1] == lane).astype(jnp.float32) for i in range(4)]
    hid = key_ref.shape[1]
    hidden = hid_ref[:, pl.ds(pl.multiple_of(at_ref[1], hid), hid)]

    def product(a, b, contract):
        dims = ((contract,), (0,)), ((), ())
        return lax.dot_general(a, b, dims, precision=HIGH, preferred_element_type=jnp.float32)

    pair_k = product(fitness * pick[0], pick[1], 0)
    pair_v = product(fitness * pick[2], pick[3], 0)
    key_ref[...] = product(bank_ref[...], product(pair_k, hidden, 1), 0)
    value_ref[...] = product(hidden, product(pair_v, bank_ref[...], 1), 0)


def cost(rows, depth, cols):
    return pl.CostEstimate(
        flops=2 * rows * depth * cols,
        bytes_accessed=2 * (rows * depth + depth * cols + rows * cols),
        transcendentals=0,
    )


def call(kernel, name, outs, specs, estimate, args, scratch=()):
    args = [pltpu.with_memory_space_constraint(a, pltpu.HBM) if s is HBM else a for a, s in zip(args, specs)]
    return pl.pallas_call(
        kernel,
        out_shape=[jax.ShapeDtypeStruct(*out) for out in outs],
        in_specs=specs,
        out_specs=[VMEM] * len(outs),
        scratch_shapes=scratch,
        compiler_params=pltpu.CompilerParams(vmem_limit_bytes=16 << 20),
        cost_estimate=estimate,
        name=name,
    )(*args)


def shards(inputs, mix, key_weight, value_weight, dim_bank, hidden_bank, member_picks, ranks):
    tok, feat = inputs.shape
    hid = key_weight.shape[1]
    half = hid // 2
    own = tok // BATCH
    core, x, z = lax.axis_index("core"), lax.axis_index("x"), lax.axis_index("z")
    block = (z * 2 + lax.axis_index("y_hi")) * hid
    at = [lax.axis_index("y_hi") * hid + core * half, block, lax.axis_index("y_low")]
    at = jnp.stack(at).astype(jnp.int32)

    key_other, value_other, bank_early = swap(key_weight), swap(value_weight), swap(dim_bank)
    scratch = [
        pltpu.SMEM(member_picks.shape, jnp.int32), pltpu.SMEM(ranks.shape, jnp.int32),
        pltpu.VMEM(inputs.shape, jnp.bfloat16), pltpu.VMEM((1, feat), jnp.float32),
        pltpu.SemaphoreType.DMA((4,)),
    ]
    shifted = call(
        functools.partial(shift_kernel, NQ), "shift", [((NQ, tok + INFO, feat), jnp.bfloat16)],
        [HBM] * 4, cost(tok, 16, feat), (member_picks, ranks, inputs, mix[None]), scratch,
    )[0]
    same = lax.all_to_all(shifted, YQ, 0, 0)
    other = beside(same)
    tokens = same, other, swap(same), swap(other)
    members = NY * own
    info = jnp.stack([t[:, tok : tok + own, :128] for t in (same, other)]).reshape(members, 128)
    ids = info[:, :4].astype(jnp.int32)

    def hidden_half(array, axis):
        return lax.dynamic_slice_in_dim(array, core * half, half, axis)

    key_pack = jnp.concatenate([hidden_half(key_weight, 1), hidden_half(key_other, 1)], axis=0)
    key_all = lax.all_gather(key_pack, "z", axis=0)
    value_pack = jnp.concatenate([hidden_half(value_weight, 0), hidden_half(value_other, 0)], axis=1)
    info = jnp.pad(info, ((0, INFO - members), (0, 2 * feat - 128)))
    value_all = lax.all_gather(jnp.concatenate([value_pack, info], axis=0), "z", axis=0)
    everyone = value_all[:, half : half + members, :128].reshape(NZ * members, 128)

    before, after = NX - 1 - x, x + 1 - 2 * lax.rem(x, 2)
    order = [x, jnp.where(core == 0, before, after), jnp.where(core == 0, after, before), lax.rem(x + 2, NX)]
    order = jnp.stack(order).astype(jnp.int32)
    deep, wide, quarter = 2 * feat, NZ * half, NY * tok // NX
    low, high = ((quarter, wide), jnp.bfloat16), ((quarter, wide), jnp.float32)
    hidden = call(
        hidden_kernel, "hidden", [((hidden_bank.shape[0], wide), jnp.float32)], [SMEM, VMEM],
        cost(hidden_bank.shape[0], 1, wide), (at, hidden_bank), [pltpu.SemaphoreType.DMA((NZ,))],
    )[0]

    def key_part(which, outs, bank_other):
        return call(
            functools.partial(key_kernel, which), "key_part", outs,
            [SMEM] * 2 + [VMEM] * 8, cost(len(which) * quarter, deep, wide),
            (order, ids, *tokens, key_all, dim_bank, bank_other, hidden),
        )

    def local(kernel, name, *args):
        return call(kernel, name, [low], [VMEM] * len(args), cost(quarter, 4, wide), args)[0]

    first = key_part((3,), [low], bank_early)[0]
    came_next = exchange(first, 0)
    bank_other = swap(call(
        copy_kernel, "bank", [(dim_bank.shape, jnp.float32)], [VMEM, ANY], cost(dim_bank.shape[0], 1, feat),
        (dim_bank, first),
    )[0])
    came_own = exchange(key_part((2,), [low], bank_other)[0], 0)
    sum_next, sum_own = key_part((1, 0), [high, high], bank_other)
    sum_next = local(add_kernel, "add", sum_next, came_next)
    other_own = exchange(sum_next, 1)
    sum_own = local(add_kernel, "add", sum_own, came_own)
    other_next = exchange(sum_own, 1)
    key_own = local(square_kernel, "square", sum_own, other_own)
    key_first = exchange(key_own, 0)
    key_next = local(square_kernel, "square", sum_next, other_next)
    keys = key_own, key_next, key_first, exchange(key_next, 0)

    def out_part(half, which, bank, kept, *done):
        out = sum(d.shape[0] for d in done) + len(which), 2, tok, feat
        return call(
            functools.partial(out_kernel, half, which), "out_part", [(out, kept)],
            [SMEM] * 2 + [VMEM] * (len(which) + 3 + len(done)), cost(len(which) * quarter, wide, feat),
            (order, ids, *[keys[i] for i in which], value_all, bank, hidden, *done),
        )[0]

    rest = out_part(1, (0, 1, 2), bank_other, jnp.bfloat16)
    came = swap(out_part(1, (3,), bank_other, jnp.bfloat16, rest))
    result = call(
        place_kernel, "place", [((NY, tok, feat), jnp.bfloat16)], [SMEM] * 2 + [VMEM] * 2,
        cost(NY * tok, 1, feat), (order, at, out_part(0, (0, 1, 2, 3), dim_bank, jnp.float32), came),
    )[0]
    result, everyone = lax.optimization_barrier((result, everyone))
    pieces = lax.all_to_all(result, YQ + ("y_low",), 0, 0)
    outputs = jnp.sum(pieces.astype(jnp.float32), axis=0).astype(jnp.bfloat16)
    key_step, value_step = call(
        step_kernel, "steps", [(key_weight.shape, jnp.float32), (value_weight.shape, jnp.float32)],
        [SMEM] + [VMEM] * 3, cost(hid, 512, feat), (at, everyone, dim_bank, hidden_bank),
    )
    return outputs, key_step, value_step


def solution(mesh):
    axes = ("z", "y_hi", "y_mid", "y_low", "x", "core")
    fine = Mesh(mesh.devices.reshape(8, 2, 2, 2, 4, 2), axes)
    pop, row, col = ("z", "y_hi"), ("y_mid", "y_low"), ("x", "core")
    in_specs = (
        P(pop + row, col),
        P(col),
        P(col, row + pop),
        P(row + pop, col),
        P(None, col),
        P(None, row),
        P(pop + row, None),
        P(pop + row),
    )
    out_specs = (P(pop + row, col), P(col, row + pop), P(row + pop, col))
    return jax.shard_map(shards, mesh=fine, in_specs=in_specs, out_specs=out_specs, check_vma=False)
```

```python
import functools

import jax
import jax.numpy as jnp
from jax import lax
from jax.experimental import pallas as pl
from jax.experimental.pallas import tpu as pltpu
from jax.sharding import Mesh
from jax.sharding import PartitionSpec as P

D = 4096
FF = 16384
BATCH = 64
MEMBERS = 128
NY, NQ = 8, 4
NX, NZ = 4, 8
INFO = 16
YQ = ("y_hi", "y_mid")
HIGH = lax.Precision.HIGHEST
SIGMA_K = 0.5 / D**0.5
SIGMA_V = 0.5 / FF**0.5
VMEM = pl.BlockSpec(memory_space=pltpu.VMEM)
HBM = pl.BlockSpec(memory_space=pltpu.HBM)
ANY = pl.BlockSpec(memory_space=pl.ANY)
SMEM = pl.BlockSpec(memory_space=pltpu.SMEM)


def swap(x):
    return lax.ppermute(x, "core", [(0, 1), (1, 0)])


def exchange(x, second):
    pairs = []
    for i in range(NX):
        for core in range(2):
            to = i ^ 1 if core == second else NX - 1 - i
            pairs.append((2 * i + core, 2 * to + core))
    return lax.ppermute(x, ("x", "core"), pairs)


def beside(x):
    pairs = []
    for y in range(NY):
        for core in range(2):
            to = y ^ 1 if core == 0 else (y + 2 * (y % 2) - 1) % NY
            pairs.append((2 * y + core, 2 * to + core))
    return lax.ppermute(x, YQ + ("y_low", "core"), pairs)


def shift_kernel(copies, picks_hbm, ranks_hbm, x_hbm, mix_hbm, out_ref, picks_ref, ranks_ref, x_ref, mix_ref, sems):
    pairs = (x_hbm, x_ref), (mix_hbm, mix_ref), (picks_hbm, picks_ref), (ranks_hbm, ranks_ref)
    fetches = [pltpu.make_async_copy(src, dst, sems.at[i]) for i, (src, dst) in enumerate(pairs)]
    for fetch in fetches:
        fetch.start()
    for fetch in fetches:
        fetch.wait()
    tok, feat = x_ref.shape
    values = x_ref[...].astype(jnp.float32)
    first = lax.broadcasted_iota(jnp.int32, values.shape, 0) % BATCH == 0
    previous = jnp.where(first, 0.0, pltpu.roll(values, 1, 0))
    shifted = (values + (previous - values) * mix_ref[...]).astype(jnp.bfloat16)
    row = lax.broadcasted_iota(jnp.int32, (INFO, feat), 0)
    lane = lax.broadcasted_iota(jnp.int32, (INFO, feat), 1)
    info = jnp.zeros((INFO, feat), jnp.float32)
    for i in range(tok // BATCH):
        entries = [picks_ref[i, j] for j in range(4)] + [ranks_ref[i]]
        for j, entry in enumerate(entries):
            info = jnp.where((row == i) & (lane == j), entry.astype(jnp.float32), info)
    info = info.astype(jnp.bfloat16)
    for i in range(copies):
        out_ref[i, :tok, :] = shifted
        out_ref[i, tok:, :] = info


def copy_kernel(x_ref, _, out_ref):
    out_ref[...] = x_ref[...]


def hidden_kernel(at_ref, hid_hbm, out_ref, sems):
    apart, width = hid_hbm.shape[1] // NZ, out_ref.shape[1] // NZ
    fetches = []
    for i in range(NZ):
        start = pl.multiple_of(at_ref[0] + i * apart, width)
        src, dst = hid_hbm.at[:, pl.ds(start, width)], out_ref.at[:, pl.ds(i * width, width)]
        fetches.append(pltpu.make_async_copy(src, dst, sems.at[i]))
        fetches[-1].start()
    for fetch in fetches:
        fetch.wait()


def key_kernel(order, order_ref, ids_ref, *refs):
    tokens, (w_ref, bank_ref, other_ref, hid_ref, *out_refs) = refs[:4], refs[4:]
    tok = tokens[0].shape[1] - INFO
    own = tok // BATCH
    blocks, inner, picks = [], [], []
    for i in order:
        u = order_ref[i]
        for s in range(2):
            for j in range(own):
                rows = [r[u, j * BATCH : (j + 1) * BATCH, :] for r in (tokens[s], tokens[2 + s])]
                m = (s * NX + u) * own + j
                fac_a = [r[pl.ds(ids_ref[m, 0], 1), :] for r in (bank_ref, other_ref)]
                dots = sum(r.astype(jnp.float32) * a for r, a in zip(rows, fac_a))
                inner.append(SIGMA_K * jnp.sum(dots, axis=1, keepdims=True))
                picks.append(ids_ref[m, 1])
                blocks.append(jnp.concatenate(rows, axis=1))
    rows = jnp.concatenate(blocks, axis=0)
    width, per = w_ref.shape[2], 2 * own
    for n in range(0, NZ, 2):
        cols = slice(n * width, (n + 2) * width)
        w = jnp.concatenate([w_ref[n], w_ref[n + 1]], axis=1)
        acc = jnp.dot(rows, w, preferred_element_type=jnp.float32)
        for k, (part, pick) in enumerate(zip(inner, picks)):
            term = acc[k * BATCH : (k + 1) * BATCH] + part * hid_ref[pl.ds(pick, 1), cols]
            i, at = divmod(k, per)
            out_refs[i][at * BATCH : (at + 1) * BATCH, cols] = term.astype(out_refs[i].dtype)


def add_kernel(kept_ref, came_ref, out_ref):
    out_ref[...] = (kept_ref[...] + came_ref[...].astype(jnp.float32)).astype(jnp.bfloat16)


def square_kernel(mine_ref, came_ref, out_ref):
    total = mine_ref[...].astype(jnp.float32) + came_ref[...].astype(jnp.float32)
    out_ref[...] = (jnp.maximum(total, 0.0) ** 2).astype(jnp.bfloat16)


def out_kernel(half, order, order_ref, ids_ref, *refs):
    keys, (v_ref, bank_ref, hid_ref, *done, out_ref) = refs[: len(order)], refs[len(order) :]
    feat, width = out_ref.shape[3], hid_ref.shape[1] // NZ
    tok = out_ref.shape[2]
    own, wide = tok // BATCH, 256
    for ref in done:
        out_ref[: ref.shape[0]] = ref[...]
    inner, picks, places = [], [], []
    for i, o in enumerate(order):
        for s in range(2):
            for j in range(own):
                m = (s * NX + order_ref[o]) * own + j
                fac_c = hid_ref[pl.ds(ids_ref[m, 2], 1), :]
                at = s * tok + j * BATCH
                part = keys[i][at : at + BATCH, :].astype(jnp.float32)
                inner.append(SIGMA_V * jnp.sum(part * fac_c, axis=1, keepdims=True))
                picks.append(ids_ref[m, 3])
                places.append((out_ref.shape[0] - len(order) + i, s, slice(j * BATCH, (j + 1) * BATCH)))
    rows = jnp.concatenate([k[...] for k in keys], axis=0)
    for n in range(feat // wide):
        cols = slice(n * wide, (n + 1) * wide)
        from_v = slice(half * feat + n * wide, half * feat + (n + 1) * wide)
        v = jnp.concatenate([v_ref[i, :width, from_v] for i in range(NZ)], axis=0)
        acc = jnp.dot(rows, v, preferred_element_type=jnp.float32)
        for k, (i, s, at) in enumerate(places):
            part = acc[k * BATCH : (k + 1) * BATCH] + inner[k] * bank_ref[pl.ds(picks[k], 1), cols]
            out_ref[i, s, at, cols] = part.astype(out_ref.dtype)


def place_kernel(order_ref, at_ref, mine_ref, came_ref, out_ref):
    twins = (0, 2, 1, 3)
    for i in range(NX):
        for s in range(2):
            total = mine_ref[i, s] + came_ref[twins[i], s].astype(jnp.float32)
            out_ref[2 * order_ref[i] + lax.rem(at_ref[2] + s, 2)] = total.astype(jnp.bfloat16)


def step_kernel(at_ref, info_ref, bank_ref, hid_ref, key_ref, value_ref):
    info = info_ref[...].astype(jnp.float32)
    fitness = 2.0 * info[:, 4:5] / (MEMBERS - 1) - 1.0
    fitness = fitness * (1.0 / MEMBERS**0.5)
    lane = lax.broadcasted_iota(jnp.int32, (info.shape[0], bank_ref.shape[0]), 1).astype(jnp.float32)
    pick = [(info[:, i : i + 1] == lane).astype(jnp.float32) for i in range(4)]
    hid = key_ref.shape[1]
    hidden = hid_ref[:, pl.ds(pl.multiple_of(at_ref[1], hid), hid)]

    def product(a, b, contract):
        dims = ((contract,), (0,)), ((), ())
        return lax.dot_general(a, b, dims, precision=HIGH, preferred_element_type=jnp.float32)

    pair_k = product(fitness * pick[0], pick[1], 0)
    pair_v = product(fitness * pick[2], pick[3], 0)
    key_ref[...] = product(bank_ref[...], product(pair_k, hidden, 1), 0)
    value_ref[...] = product(hidden, product(pair_v, bank_ref[...], 1), 0)


def cost(rows, depth, cols):
    return pl.CostEstimate(
        flops=2 * rows * depth * cols,
        bytes_accessed=2 * (rows * depth + depth * cols + rows * cols),
        transcendentals=0,
    )


def call(kernel, name, outs, specs, estimate, args, scratch=()):
    args = [pltpu.with_memory_space_constraint(a, pltpu.HBM) if s is HBM else a for a, s in zip(args, specs)]
    return pl.pallas_call(
        kernel,
        out_shape=[jax.ShapeDtypeStruct(*out) for out in outs],
        in_specs=specs,
        out_specs=[VMEM] * len(outs),
        scratch_shapes=scratch,
        compiler_params=pltpu.CompilerParams(vmem_limit_bytes=10 << 20),
        cost_estimate=estimate,
        name=name,
    )(*args)


def shards(inputs, mix, key_weight, value_weight, dim_bank, hidden_bank, member_picks, ranks):
    tok, feat = inputs.shape
    hid = key_weight.shape[1]
    half = hid // 2
    own = tok // BATCH
    core, x, z = lax.axis_index("core"), lax.axis_index("x"), lax.axis_index("z")
    block = (z * 2 + lax.axis_index("y_hi")) * hid
    at = [lax.axis_index("y_hi") * hid + core * half, block, lax.axis_index("y_low")]
    at = jnp.stack(at).astype(jnp.int32)

    key_other, value_other, bank_early = swap(key_weight), swap(value_weight), swap(dim_bank)
    scratch = [
        pltpu.SMEM(member_picks.shape, jnp.int32), pltpu.SMEM(ranks.shape, jnp.int32),
        pltpu.VMEM(inputs.shape, jnp.bfloat16), pltpu.VMEM((1, feat), jnp.float32),
        pltpu.SemaphoreType.DMA((4,)),
    ]
    shifted = call(
        functools.partial(shift_kernel, NQ), "shift", [((NQ, tok + INFO, feat), jnp.bfloat16)],
        [HBM] * 4, cost(tok, 16, feat), (member_picks, ranks, inputs, mix[None]), scratch,
    )[0]
    same = lax.all_to_all(shifted, YQ, 0, 0)
    other = beside(same)
    tokens = same, other, swap(same), swap(other)
    members = NY * own
    info = jnp.stack([t[:, tok : tok + own, :128] for t in (same, other)]).reshape(members, 128)
    ids = info[:, :4].astype(jnp.int32)

    def hidden_half(array, axis):
        return lax.dynamic_slice_in_dim(array, core * half, half, axis)

    key_pack = jnp.concatenate([hidden_half(key_weight, 1), hidden_half(key_other, 1)], axis=0)
    key_all = lax.all_gather(key_pack, "z", axis=0)
    value_pack = jnp.concatenate([hidden_half(value_weight, 0), hidden_half(value_other, 0)], axis=1)
    info = jnp.pad(info, ((0, INFO - members), (0, 2 * feat - 128)))
    value_all = lax.all_gather(jnp.concatenate([value_pack, info], axis=0), "z", axis=0)
    everyone = value_all[:, half : half + members, :128].reshape(NZ * members, 128)

    before, after = NX - 1 - x, x + 1 - 2 * lax.rem(x, 2)
    order = [x, jnp.where(core == 0, before, after), jnp.where(core == 0, after, before), lax.rem(x + 2, NX)]
    order = jnp.stack(order).astype(jnp.int32)
    deep, wide, quarter = 2 * feat, NZ * half, NY * tok // NX
    low, high = ((quarter, wide), jnp.bfloat16), ((quarter, wide), jnp.float32)
    hidden = call(
        hidden_kernel, "hidden", [((hidden_bank.shape[0], wide), jnp.float32)], [SMEM, VMEM],
        cost(hidden_bank.shape[0], 1, wide), (at, hidden_bank), [pltpu.SemaphoreType.DMA((NZ,))],
    )[0]

    def key_part(which, outs, bank_other):
        return call(
            functools.partial(key_kernel, which), "key_part", outs,
            [SMEM] * 2 + [VMEM] * 8, cost(len(which) * quarter, deep, wide),
            (order, ids, *tokens, key_all, dim_bank, bank_other, hidden),
        )

    def local(kernel, name, *args):
        return call(kernel, name, [low], [VMEM] * len(args), cost(quarter, 4, wide), args)[0]

    first = key_part((3,), [low], bank_early)[0]
    came_next = exchange(first, 0)
    bank_other = swap(call(
        copy_kernel, "bank", [(dim_bank.shape, jnp.float32)], [VMEM, ANY], cost(dim_bank.shape[0], 1, feat),
        (dim_bank, first),
    )[0])
    came_own = exchange(key_part((2,), [low], bank_other)[0], 0)
    sum_next, sum_own = key_part((1, 0), [high, high], bank_other)
    sum_next = local(add_kernel, "add", sum_next, came_next)
    other_own = exchange(sum_next, 1)
    sum_own = local(add_kernel, "add", sum_own, came_own)
    other_next = exchange(sum_own, 1)
    key_own = local(square_kernel, "square", sum_own, other_own)
    key_first = exchange(key_own, 0)
    key_next = local(square_kernel, "square", sum_next, other_next)
    keys = key_own, key_next, key_first, exchange(key_next, 0)

    def out_part(half, which, bank, kept, *done):
        out = sum(d.shape[0] for d in done) + len(which), 2, tok, feat
        return call(
            functools.partial(out_kernel, half, which), "out_part", [(out, kept)],
            [SMEM] * 2 + [VMEM] * (len(which) + 3 + len(done)), cost(len(which) * quarter, wide, feat),
            (order, ids, *[keys[i] for i in which], value_all, bank, hidden, *done),
        )[0]

    rest = out_part(1, (0, 1, 2), bank_other, jnp.bfloat16)
    came = swap(out_part(1, (3,), bank_other, jnp.bfloat16, rest))
    result = call(
        place_kernel, "place", [((NY, tok, feat), jnp.bfloat16)], [SMEM] * 2 + [VMEM] * 2,
        cost(NY * tok, 1, feat), (order, at, out_part(0, (0, 1, 2, 3), dim_bank, jnp.float32), came),
    )[0]
    result, everyone = lax.optimization_barrier((result, everyone))
    pieces = lax.all_to_all(result, YQ + ("y_low",), 0, 0)
    outputs = jnp.sum(pieces.astype(jnp.float32), axis=0).astype(jnp.bfloat16)
    key_step, value_step = call(
        step_kernel, "steps", [(key_weight.shape, jnp.float32), (value_weight.shape, jnp.float32)],
        [SMEM] + [VMEM] * 3, cost(hid, 512, feat), (at, everyone, dim_bank, hidden_bank),
    )
    return outputs, key_step, value_step


def solution(mesh):
    axes = ("z", "y_hi", "y_mid", "y_low", "x", "core")
    fine = Mesh(mesh.devices.reshape(8, 2, 2, 2, 4, 2), axes)
    pop, row, col = ("z", "y_hi"), ("y_mid", "y_low"), ("x", "core")
    in_specs = (
        P(pop + row, col),
        P(col),
        P(col, row + pop),
        P(row + pop, col),
        P(None, col),
        P(None, row),
        P(pop + row, None),
        P(pop + row),
    )
    out_specs = (P(pop + row, col), P(col, row + pop), P(row + pop, col))
    return jax.shard_map(shards, mesh=fine, in_specs=in_specs, out_specs=out_specs, check_vma=False)
```
